512 devices in a mesh: seg: 32 (over z_lo, x), bank: 16 (over y, z_hi, core).
Axes of the slice: x: 4, y: 4, z: 16 (z_hi: 2, z_lo: 8; z = z_hi * 8 + z_lo), core: 2. Of those that a mesh axis runs over, the one named last changes fastest.
Arguments:
- strain: float32 [1572864], P('seg'), may hold values from -24000 to 24000, as said below
- inv_asd: float32 [32768], replicated, may hold values from 0.3 to 3
- templates: bfloat16 [2, 32, 32768], P(None, 'bank'), may hold values from -6 to 6
- tmpl_len: int32 [32], P('bank'), may hold values from 2048 to 16384, as said below
- weights: float32 [32], P('bank'), may hold values from 0.2 to 5
- chirp_mass: float32 [32], P('bank'), may hold values from 10 to 60
- valid: int32 [1536], P('seg'), may hold values 0 or 1
Outputs:
- log_like: float32 [1572864], P(('seg', 'bank'))
- chirp_mean: float32 [1572864], P(('seg', 'bank'))
- delay_mean: float32 [1572864], P(('seg', 'bank'))
The draws below stay inside these ranges and needn't reach their ends.
Inputs may be any that keep to these rules, and one draw needn't show every extreme that they name: `strain`: noise amplitude may change from one block of 1024 samples to the next. `tmpl_len`: template lengths lie between 2048 and 16384 samples, both ends taken.
All inputs are finite; a program needn't handle non-finite values. No bound on the sum of `valid` on one device may be relied on, other than what follows from the above.
Results may differ from the reference program's by a relative error of at most 0.00035.
Values sent between devices are 32-bit elements; how exact they have to be, the bound alone decides.
A program may use at most 64 MiB of HBM per device.

```python
import math
import jax
import jax.numpy as jnp
from jax import lax

NFFT = 65536
OVER = 16384
GATE = 1024
RATE = 4096
NBIN = 32768
HOP = 49152
TEMPLATES = 32
SAMPLES = 1572864


def draw_strain(key, part):
    noise_key, level_key = jax.random.split(key, 2)
    block_count = SAMPLES // GATE
    noise = jnp.clip(jax.random.normal(noise_key, (SAMPLES,), jnp.float32), -8.0, 8.0)
    envelope = jnp.exp(jax.random.uniform(level_key, (block_count,), jnp.float32, math.log(0.5), math.log(2.0)))
    return (noise.reshape(block_count, GATE) * envelope[:, None]).reshape(SAMPLES)


def draw_tmpl_len(key, part):
    first_key, top_key, low_key = jax.random.split(jax.random.fold_in(key, 17), 3)
    lengths = jax.random.randint(first_key, (TEMPLATES,), OVER // 8, OVER + 1, jnp.int32)
    top_index = jax.random.randint(top_key, (), 0, TEMPLATES, jnp.int32)
    low_index = (top_index + 1 + jax.random.randint(low_key, (), 0, TEMPLATES - 1, jnp.int32)) % TEMPLATES
    positions = jnp.arange(TEMPLATES, dtype=jnp.int32)
    lengths = jnp.where(positions == top_index, OVER, lengths)
    lengths = jnp.where(positions == low_index, OVER // 8, lengths)
    return lengths.astype(jnp.int32)


def plant(values, key, smallest, high):
    dims = values.shape
    place = [jax.random.randint(jax.random.fold_in(key, axis), (), 0, dims[axis]) for axis in range(len(dims))]
    values = values.at[tuple(place)].set(smallest)
    longest = dims.index(max(dims))
    place[longest] = (place[longest] + 1) % dims[longest]
    return values.at[tuple(place)].set(high)


def block_scale(stream_key, dims, cuts, smallest, top_value):
    gain = 1.0
    for position, parts in cuts:
        steps = jax.random.uniform(jax.random.fold_in(jax.random.fold_in(stream_key, 6), position), (parts,), jnp.float32, smallest / len(cuts), top_value / len(cuts))
        gain = gain * jnp.repeat(jnp.exp(steps), dims[position] // parts).reshape((-1,) + (1,) * (len(dims) - 1 - position))
    return gain


def gaussian(key, shape, scale, limit, pieces=(), kind=jnp.bfloat16):
    result = jax.random.normal(key, shape, jnp.float32) * scale
    if len(pieces) > 0:
        result = block_scale(key, shape, pieces, -0.22, 0.18) * result
    return jnp.clip(result, min=-limit, max=limit).astype(kind)


def setup_inputs(seed: int = 0) -> dict:
    key_of = jax.random.split(jax.random.key(seed), 8)
    return {
        "strain": draw_strain(jax.random.fold_in(key_of[7], 71), 0),
        "inv_asd": jnp.clip(jnp.exp(jax.random.uniform(key_of[1], (NBIN,), jnp.float32, math.log(0.3), math.log(3.0))), 0.3, 3.0),
        "templates": gaussian(key_of[2], (2, TEMPLATES, NBIN), 1.0, 6.0, ((1, 16),)),
        "tmpl_len": draw_tmpl_len(jax.random.fold_in(key_of[7], 71), 0),
        "weights": jnp.clip(jnp.exp(math.log(5.0) - 3.218876 * jax.random.uniform(key_of[4], (TEMPLATES,), jnp.float32) ** block_scale(key_of[4], (TEMPLATES,), ((0, 16),), -0.2, 0.2)), 0.2, 5.0),
        "chirp_mass": jnp.clip(jnp.exp(math.log(60.0) - 1.7917595 * jax.random.uniform(key_of[5], (TEMPLATES,), jnp.float32) ** block_scale(key_of[5], (TEMPLATES,), ((0, 16),), -0.2, 0.2)), 10.0, 60.0),
        "valid": plant((jax.random.randint(key_of[6], (SAMPLES // GATE,), 0, 8) < 7).astype(jnp.int32), jax.random.fold_in(key_of[6], 1), 0, 1),
    }


def log_bessel(rho_val):
    small_x = jnp.minimum(rho_val, 3.75)
    small_t = (small_x / 3.75) ** 2
    small_poly = 1.0 + small_t * (3.5156229 + small_t * (3.0899424 + small_t * (1.2067492 + small_t * (0.2659732 + small_t * (0.0360768 + small_t * 0.0045813)))))
    large_x = jnp.maximum(rho_val, 3.75)
    large_q = 3.75 / large_x
    large_poly = 0.39894228 + large_q * (0.01328592 + large_q * (0.00225319 + large_q * (-0.00157565 + large_q * (0.00916281 + large_q * (-0.02057706 + large_q * (0.02635537 + large_q * (-0.01647633 + large_q * 0.00392377)))))))
    large_val = large_x - 0.5 * jnp.log(large_x) + jnp.log(large_poly)
    return jnp.where(rho_val < 3.75, jnp.log(small_poly), large_val)

def reference(strain, inv_asd, templates, tmpl_len, weights, chirp_mass, valid):
    gate_mask = jnp.repeat(valid.astype(strain.dtype), GATE)
    gated_data = strain * gate_mask
    padded = jnp.concatenate([jnp.zeros((OVER,), strain.dtype), gated_data])
    tmpl_re = templates[0].astype(jnp.float32)
    tmpl_im = templates[1].astype(jnp.float32)
    sigma_sq = lax.optimization_barrier(jnp.sum((inv_asd * inv_asd)[None, :] * (tmpl_re * tmpl_re + tmpl_im * tmpl_im), axis=1))
    starts = (OVER - tmpl_len).astype(jnp.int32)
    delays = tmpl_len.astype(jnp.float32) / RATE
    prior_sum = jnp.sum(weights)

    def pick_row(score_row, begin_at):
        return lax.dynamic_slice_in_dim(score_row, begin_at, HOP)

    def per_segment(segment):
        window = lax.dynamic_slice_in_dim(padded, segment * HOP, NFFT)
        spectrum = jnp.fft.fft(window)[:NBIN] * inv_asd / math.sqrt(NFFT)
        spec_re = jnp.real(spectrum)
        spec_im = jnp.imag(spectrum)
        prod_re = spec_re[None, :] * tmpl_re + spec_im[None, :] * tmpl_im
        prod_im = spec_im[None, :] * tmpl_re - spec_re[None, :] * tmpl_im
        padded_bins = jnp.pad(prod_re + 1j * prod_im, ((0, 0), (0, NFFT - NBIN)))
        corr = jnp.fft.ifft(padded_bins, axis=1) * NFFT
        power = jnp.real(corr) ** 2 + jnp.imag(corr) ** 2
        rho_val = jnp.sqrt(power / sigma_sq[:, None])
        scores = log_bessel(rho_val)
        aligned = jax.vmap(pick_row)(scores, starts)
        peak_score = lax.optimization_barrier(jnp.max(aligned, axis=0))
        masses = weights[:, None] * jnp.exp(aligned - peak_score[None, :])
        total = lax.optimization_barrier(jnp.sum(masses, axis=0))
        chirp_sum = lax.optimization_barrier(jnp.sum(masses * chirp_mass[:, None], axis=0))
        delay_sum = lax.optimization_barrier(jnp.sum(masses * delays[:, None], axis=0))
        return (peak_score + jnp.log(total) - jnp.log(prior_sum), chirp_sum / total, delay_sum / total)
    segments = jnp.arange(SAMPLES // HOP, dtype=jnp.int32)
    log_like, chirp_mean, delay_mean = lax.map(per_segment, segments)
    return (log_like.reshape(-1), chirp_mean.reshape(-1), delay_mean.reshape(-1))
```

```python
import functools
import math

import jax
import jax.numpy as jnp
import ml_dtypes
import numpy as np
from jax import lax
from jax.experimental import pallas as pl
from jax.experimental.pallas import tpu as pltpu
from jax.sharding import PartitionSpec as P

NFFT = 65536
OVER = 16384
RATE = 4096
HOP = 49152
F32, BF16 = jnp.float32, jnp.bfloat16
MESH = pl.DeviceIdType.MESH
CHUNKS = 3
GROUP = 8


def halves(table):
    high = table.astype(ml_dtypes.bfloat16)
    low = (table - high.astype(np.float64)).astype(ml_dtypes.bfloat16)
    return high, low


@functools.cache
def tables():
    turn = np.outer(np.arange(256), np.arange(256)) % 256 * (2 * np.pi / 256)
    cos, sin = np.cos(turn), np.sin(turn)
    first = np.concatenate([cos, -sin])
    high, low = halves(first)
    own = np.concatenate(
        [high[:, 64:], low[:, 64:], high[:, 64:], np.zeros_like(high[:, :64])], axis=1
    )
    halo = np.concatenate(
        [high[:, :64], low[:, :64], high[:, :64], np.zeros_like(high[:, :64])], axis=1
    )
    second = np.stack(halves(np.block([[cos[:128], sin[:128]], [-sin[:128], cos[:128]]])))
    third = np.stack(halves(np.block([[cos[:, :128], -sin[:, :128]], [sin[:, :128], cos[:, :128]]])))
    order = np.array(
        [
            48 * y + 24 * z + 12 * core + 4 * j + i
            for j in range(3)
            for y in range(4)
            for core in range(2)
            for z in range(2)
            for i in range(4)
        ]
    )
    cos_t, sin_t = cos[order], sin[order]
    fourth = np.stack(halves(np.block([[cos_t, -sin_t], [sin_t, cos_t]])))
    twist = np.outer(np.arange(256), np.arange(256)) * (2 * np.pi / NFFT)
    twist = np.stack([np.cos(twist), np.sin(twist)]).astype(np.float32)
    pick = np.zeros((512, 512), ml_dtypes.bfloat16)
    for k in range(2):
        for h in range(2):
            for a in range(128):
                pick[k * 256 + h * 128 + a, (2 * a + h) * 2 + k] = 1
    return own, halo, second, third, fourth, twist, pick


def split(value):
    high = value.astype(BF16)
    return high, (value - high.astype(F32)).astype(BF16)


def mul(left, right):
    return lax.dot_general(left, right, (((1,), (0,)), ((), ())), preferred_element_type=F32)


def mul_t(left, right):
    return lax.dot_general(left, right, (((1,), (1,)), ((), ())), preferred_element_type=F32)


def cos_sin_turn(fraction):
    half = (fraction - jnp.where(fraction >= 0.5, 1.0, 0.0)) * math.pi
    sq = half * half
    s = 1.0 / 6227020800.0
    for term in (-1.0 / 39916800.0, 1.0 / 362880.0, -1.0 / 5040.0, 1.0 / 120.0, -1.0 / 6.0, 1.0):
        s = s * sq + term
    s = s * half
    c = -1.0 / 87178291200.0
    for term in (
        1.0 / 479001600.0,
        -1.0 / 3628800.0,
        1.0 / 40320.0,
        -1.0 / 720.0,
        1.0 / 24.0,
        -0.5,
        1.0,
    ):
        c = c * sq + term
    return 1.0 - 2.0 * s * s, 2.0 * s * c


def log_bessel(power):
    edge = 3.75 * 3.75
    t = jnp.minimum(power, edge) * (1.0 / edge)
    small = jnp.full_like(t, 0.0045813)
    for term in (0.0360768, 0.2659732, 1.2067492, 3.0899424, 3.5156229, 1.0):
        small = small * t + term
    above = jnp.maximum(power, edge)
    inverse = lax.rsqrt(above)
    x = above * inverse
    q = 3.75 * inverse
    large = jnp.full_like(t, 0.00392377)
    for term in (
        -0.01647633,
        0.02635537,
        -0.02057706,
        0.00916281,
        -0.00157565,
        0.00225319,
        0.01328592,
        0.39894228,
    ):
        large = large * q + term
    is_small = power < edge
    return jnp.where(is_small, 0.0, x) + jnp.log(
        jnp.where(is_small, small, large * lax.rsqrt(x))
    )


def kernel(
    strain_hbm, asd_hbm, tmpl_hbm, own_hbm, halo_hbm, second_hbm, third_hbm, fourth_hbm, twist_hbm, pick_hbm,
    len_ref, weight_ref, mass_ref, valid_ref,
    log_ref, chirp_ref, delay_ref,
    strain, asd, tmpl, own_w, halo_w, second_w, third_w, fourth_w, twist, pick,
    gated, halo, filt, corr, send, recv, trait, traits, prior, priors, zsend, zrecv, zown,
    in_sem, halo_sem, send_sem, recv_sem, trait_send, trait_recv, prior_sem, zsend_sem, zrecv_sem,
):
    seg, bank = lax.axis_index("seg"), lax.axis_index("bank")
    seg_count = lax.axis_size("seg")
    y, z, core = bank // 4, bank // 2 % 2, bank % 2
    rank = y * 2 + core

    def bank_of(rank_, z_):
        return rank_ // 2 * 4 + z_ * 2 + rank_ % 2

    sources = (strain_hbm, asd_hbm, tmpl_hbm, pick_hbm, own_hbm, twist_hbm, halo_hbm, second_hbm, third_hbm, fourth_hbm)
    targets = (strain, asd, tmpl, pick, own_w, twist, halo_w, second_w, third_w, fourth_w)
    loads = [
        pltpu.make_async_copy(source, target, in_sem.at[i])
        for i, (source, target) in enumerate(zip(sources, targets))
    ]
    for load in loads:
        load.start()

    barrier = pltpu.get_barrier_semaphore()

    @pl.when(seg > 0)
    def _():
        pl.semaphore_signal(barrier, inc=1, device_id=(seg - 1, bank), device_id_type=MESH)

    peers = [(seg, bank_of((rank + o) % GROUP, z)) for o in range(1, GROUP)]
    opposite = (seg, bank_of(rank, 1 - z))
    for peer in peers + [opposite]:
        pl.semaphore_signal(barrier, inc=1, device_id=peer, device_id_type=MESH)

    row = lax.broadcasted_iota(jnp.int32, (8, 128), 0)
    facts = (
        weight_ref[0] + weight_ref[1],
        mass_ref[0],
        mass_ref[1],
        len_ref[0].astype(F32) * (1.0 / RATE),
        len_ref[1].astype(F32) * (1.0 / RATE),
    )
    tile = jnp.zeros((8, 128), F32)
    for i, fact in enumerate(facts):
        tile = jnp.where(row == i, fact, tile)
    trait[...] = tile

    loads[0].wait()
    for i in range(47, -1, -1):
        gated[8 * i : 8 * i + 8, :] = strain[8 * i : 8 * i + 8, :] * valid_ref[i].astype(F32)

    pl.semaphore_wait(barrier, GROUP + 1 - (seg + 1) // seg_count)

    def halo_copy():
        return pltpu.make_async_remote_copy(
            src_ref=gated.at[256:384], dst_ref=halo, send_sem=halo_sem.at[0], recv_sem=halo_sem.at[1],
            device_id=(seg + 1, bank), device_id_type=MESH,
        )

    @pl.when(seg < seg_count - 1)
    def _():
        halo_copy().start()

    @pl.when(seg == 0)
    def _():
        halo[...] = jnp.zeros((128, 128), F32)

    trait_copies = [
        pltpu.make_async_remote_copy(
            src_ref=trait, dst_ref=traits.at[o], send_sem=trait_send.at[o], recv_sem=trait_recv.at[o],
            device_id=peers[o - 1], device_id_type=MESH,
        )
        for o in range(1, GROUP)
    ]
    for copy in trait_copies:
        copy.start()

    def frame(ref, begin, count):
        return jnp.concatenate(
            [ref[pl.ds(begin, count, 2), :], ref[pl.ds(begin + 1, count, 2), :]], axis=1
        )

    high, low = split(frame(gated, 0, 192))
    loads[4].wait()
    blank = jnp.zeros((64, 256), BF16)
    part = mul(own_w[...], jnp.concatenate([high, high, low, blank], axis=0))

    loads[1].wait()
    loads[2].wait()
    loads[3].wait()
    level = frame(asd, 0, 128)
    deal = mul(pick[...], jnp.concatenate([tmpl[0], tmpl[1]], axis=1))
    for k in range(2):
        parts = [deal[256 * k + 128 * h : 256 * k + 128 * h + 128] for h in range(2)]
        tmpl_re = jnp.concatenate([p[:, :128] for p in parts], axis=1)
        tmpl_im = jnp.concatenate([p[:, 128:] for p in parts], axis=1)
        sigma = jnp.sum(level * level * (tmpl_re * tmpl_re + tmpl_im * tmpl_im), keepdims=True)
        start = OVER - len_ref[k]
        index = lax.broadcasted_iota(jnp.int32, (128, 128), 0) * start % 256
        long_cos, long_sin = cos_sin_turn(index.astype(F32) * (1.0 / 256))
        index = lax.broadcasted_iota(jnp.int32, (1, 256), 1) * start % NFFT
        short_cos, short_sin = cos_sin_turn(index.astype(F32) * (1.0 / NFFT))
        long_cos = jnp.concatenate([long_cos, long_cos], axis=1)
        long_sin = jnp.concatenate([long_sin, long_sin], axis=1)
        turn_re = long_cos * short_cos - long_sin * short_sin
        turn_im = long_cos * short_sin + long_sin * short_cos
        scale = level * (lax.rsqrt(sigma) * (1.0 / math.sqrt(NFFT)))
        filt[k, 0] = (tmpl_re * turn_re + tmpl_im * turn_im) * scale
        filt[k, 1] = (tmpl_re * turn_im - tmpl_im * turn_re) * scale

    @pl.when(seg > 0)
    def _():
        halo_copy().wait_recv()

    loads[6].wait()
    high, low = split(frame(halo, 0, 64))
    part = part + mul(halo_w[...], jnp.concatenate([high, high, low, blank], axis=0))
    loads[5].wait()
    twist_cos, twist_sin = twist[0], twist[1]
    turned = jnp.concatenate(
        [
            part[:256] * twist_cos + part[256:] * twist_sin,
            part[256:] * twist_cos - part[:256] * twist_sin,
        ],
        axis=1,
    )
    high, low = split(turned)
    loads[7].wait()
    spec = mul_t(
        jnp.concatenate([second_w[0], second_w[1], second_w[0]], axis=1),
        jnp.concatenate([high, high, low], axis=1),
    )
    spec_re, spec_im = spec[:128], spec[128:]
    prods = []
    for k in range(2):
        filt_re, filt_im = filt[k, 0], filt[k, 1]
        prods.append(
            jnp.concatenate(
                [spec_re * filt_re - spec_im * filt_im, spec_re * filt_im + spec_im * filt_re], axis=0
            )
        )
    loads[8].wait()
    loads[9].wait()
    third = jnp.concatenate([third_w[0], third_w[1], third_w[0]], axis=1)
    fourth = jnp.concatenate([fourth_w[0], fourth_w[1], fourth_w[0]], axis=1)
    for k in range(2):
        high, low = split(prods[k])
        inner = mul(third, jnp.concatenate([high, high, low], axis=0))
        turned = jnp.concatenate(
            [
                inner[:256] * twist_cos - inner[256:] * twist_sin,
                inner[:256] * twist_sin + inner[256:] * twist_cos,
            ],
            axis=1,
        )
        high, low = split(turned)
        corr[k] = mul_t(fourth, jnp.concatenate([high, high, low], axis=1))

    def score_copy(j, o):
        return pltpu.make_async_remote_copy(
            src_ref=send.at[j, (rank + o) % GROUP], dst_ref=recv.at[j, o],
            send_sem=send_sem.at[j, o], recv_sem=recv_sem.at[j, o],
            device_id=(seg, bank_of((rank + o) % GROUP, z)), device_id_type=MESH,
        )

    log_weight = [jnp.log(jnp.full((8, 256), weight_ref[k], F32)) for k in range(2)]
    for j in range(CHUNKS):
        for o in (4, 5, 3, 2, 6, 7, 1, 0):
            dest = (rank + o) % GROUP
            begin = pl.multiple_of(j * 64 + dest * 8, 8)
            for k in range(2):
                re = corr[k, pl.ds(begin, 8), :]
                im = corr[k, pl.ds(begin + 192, 8), :]
                send[j, dest, k] = log_bessel(re * re + im * im) + log_weight[k]
            if o:
                score_copy(j, o).start()

    for copy in trait_copies:
        copy.wait_recv()
    traits[0] = trait[...]
    weight_sum = traits[0, 0:1, :]
    for o in range(1, GROUP):
        weight_sum = weight_sum + traits[o, 0:1, :]
    prior[...] = jnp.broadcast_to(weight_sum, (8, 128))
    prior_copy = pltpu.make_async_remote_copy(
        src_ref=prior, dst_ref=priors, send_sem=prior_sem.at[0], recv_sem=prior_sem.at[1],
        device_id=opposite, device_id_type=MESH,
    )
    prior_copy.start()

    def z_copy(j):
        return pltpu.make_async_remote_copy(
            src_ref=zsend.at[j], dst_ref=zrecv.at[j], send_sem=zsend_sem.at[j], recv_sem=zrecv_sem.at[j],
            device_id=opposite, device_id_type=MESH,
        )

    for j in range(CHUNKS):
        for o in range(1, GROUP):
            score_copy(j, o).wait_recv()
        scores = [send[j, rank, k] for k in range(2)]
        for o in range(1, GROUP):
            scores += [recv[j, o, k] for k in range(2)]
        peak = functools.reduce(jnp.maximum, scores)
        total = chirp_sum = delay_sum = jnp.zeros((8, 256), F32)
        for i, score in enumerate(scores):
            o, k = divmod(i, 2)
            mass = jnp.exp(score - peak)
            total = total + mass
            chirp_sum = chirp_sum + mass * traits[o, 1 + k : 2 + k, 0:1]
            delay_sum = delay_sum + mass * traits[o, 3 + k : 4 + k, 0:1]
        inverse = 1.0 / total
        for i, value in enumerate((peak + jnp.log(total), chirp_sum * inverse, delay_sum * inverse)):
            rows = [
                jnp.concatenate([value[4 * h : 4 * h + 4, :128], value[4 * h : 4 * h + 4, 128:]], axis=0)
                for h in range(2)
            ]
            zown[j, 8 * i : 8 * i + 8] = jnp.where(z == 0, rows[0], rows[1])
            zsend[j, 8 * i : 8 * i + 8] = jnp.where(z == 0, rows[1], rows[0])
        z_copy(j).start()

    prior_copy.wait_recv()
    log_prior = jnp.log(prior[...] + priors[...])
    for j in range(CHUNKS):
        z_copy(j).wait_recv()
        mine, other = zown[j], zrecv[j]
        peak = jnp.maximum(mine[:8], other[:8])
        mass_a, mass_b = jnp.exp(mine[:8] - peak), jnp.exp(other[:8] - peak)
        total = mass_a + mass_b
        inverse = 1.0 / total
        values = (
            peak + jnp.log(total) - log_prior,
            (mass_a * mine[8:16] + mass_b * other[8:16]) * inverse,
            (mass_a * mine[16:] + mass_b * other[16:]) * inverse,
        )
        for out, value in zip((log_ref, chirp_ref, delay_ref), values):
            for h in range(2):
                out[pl.ds(8 * j + h, 4, 2), :] = value[4 * h : 4 * h + 4]

    @pl.when(seg < seg_count - 1)
    def _():
        halo_copy().wait_send()

    for copy in trait_copies + [prior_copy]:
        copy.wait_send()
    for j in range(CHUNKS):
        for o in range(1, GROUP):
            score_copy(j, o).wait_send()
        z_copy(j).wait_send()


def local(strain, inv_asd, templates, tmpl_len, weights, chirp_mass, valid):
    own, halo, second, third, fourth, twist, pick = tables()
    dealt = templates.reshape(2, 2, 256, 128).transpose(0, 2, 1, 3).reshape(2, 512, 128)
    anywhere = pl.BlockSpec(memory_space=pl.ANY)
    scalars = pl.BlockSpec(memory_space=pltpu.SMEM)
    held = pl.BlockSpec(memory_space=pltpu.VMEM)
    dma = pltpu.SemaphoreType.DMA
    share = jax.ShapeDtypeStruct((24, 128), F32)
    outs = pl.pallas_call(
        kernel,
        out_shape=(share, share, share),
        in_specs=[anywhere] * 10 + [scalars] * 4,
        out_specs=(held, held, held),
        scratch_shapes=[
            pltpu.VMEM((384, 128), F32),
            pltpu.VMEM((256, 128), F32),
            pltpu.VMEM((2, 512, 128), BF16),
            pltpu.VMEM(own.shape, BF16),
            pltpu.VMEM(halo.shape, BF16),
            pltpu.VMEM(second.shape, BF16),
            pltpu.VMEM(third.shape, BF16),
            pltpu.VMEM(fourth.shape, BF16),
            pltpu.VMEM(twist.shape, F32),
            pltpu.VMEM(pick.shape, BF16),
            pltpu.VMEM((384, 128), F32),
            pltpu.VMEM((128, 128), F32),
            pltpu.VMEM((2, 2, 128, 256), F32),
            pltpu.VMEM((2, 384, 256), F32),
            pltpu.VMEM((CHUNKS, GROUP, 2, 8, 256), F32),
            pltpu.VMEM((CHUNKS, GROUP, 2, 8, 256), F32),
            pltpu.VMEM((8, 128), F32),
            pltpu.VMEM((GROUP, 8, 128), F32),
            pltpu.VMEM((8, 128), F32),
            pltpu.VMEM((8, 128), F32),
            pltpu.VMEM((CHUNKS, 24, 128), F32),
            pltpu.VMEM((CHUNKS, 24, 128), F32),
            pltpu.VMEM((CHUNKS, 24, 128), F32),
            dma((10,)),
            dma((2,)),
            dma((CHUNKS, GROUP)),
            dma((CHUNKS, GROUP)),
            dma((GROUP,)),
            dma((GROUP,)),
            dma((2,)),
            dma((CHUNKS,)),
            dma((CHUNKS,)),
        ],
        compiler_params=pltpu.CompilerParams(
            collective_id=0, has_side_effects=True, vmem_limit_bytes=60 * 1024 * 1024
        ),
    )(
        strain.reshape(384, 128), inv_asd.reshape(256, 128), dealt,
        own, halo, second, third, fourth, twist, pick,
        tmpl_len, weights, chirp_mass, valid,
    )
    return tuple(out.reshape(3072) for out in outs)


def solution(mesh):
    placed = (P("seg"), P(), P(None, "bank", None), P("bank"), P("bank"), P("bank"), P("seg"))
    return jax.shard_map(
        local,
        mesh=mesh,
        in_specs=placed,
        out_specs=(P(("seg", "bank")), P(("seg", "bank")), P(("seg", "bank"))),
        check_vma=False,
    )
```

```python
import functools
import math

import jax
import jax.numpy as jnp
import ml_dtypes
import numpy as np
from jax import lax
from jax.experimental import pallas as pl
from jax.experimental.pallas import tpu as pltpu
from jax.sharding import PartitionSpec as P

NFFT = 65536
OVER = 16384
RATE = 4096
HOP = 49152
F32, BF16 = jnp.float32, jnp.bfloat16
MESH = pl.DeviceIdType.MESH
CHUNKS = 3
GROUP = 8


def halves(table):
    high = table.astype(ml_dtypes.bfloat16)
    low = (table - high.astype(np.float64)).astype(ml_dtypes.bfloat16)
    return high, low


@functools.cache
def tables():
    turn = np.outer(np.arange(256), np.arange(256)) % 256 * (2 * np.pi / 256)
    base = np.stack(halves(np.concatenate([np.cos(turn), np.sin(turn)])))
    order = np.array(
        [
            48 * y + 24 * z + 12 * core + 4 * j + i
            for j in range(3)
            for y in range(4)
            for core in range(2)
            for z in range(2)
            for i in range(4)
        ]
    )
    last = np.stack(halves(np.concatenate([np.cos(turn)[order], np.sin(turn)[order]])))
    twist = np.outer(np.arange(256), np.arange(256)) * (2 * np.pi / NFFT)
    twist = np.stack([np.cos(twist), np.sin(twist)]).astype(np.float32)
    pick = np.zeros((128, 128), ml_dtypes.bfloat16)
    for k in range(2):
        for h in range(2):
            for a in range(32):
                pick[k * 64 + h * 32 + a, (2 * a + h) * 2 + k] = 1
    return base, last, twist, pick


def split(value):
    high = value.astype(BF16)
    return high, (value - high.astype(F32)).astype(BF16)


def mul(left, right):
    return lax.dot_general(left, right, (((1,), (0,)), ((), ())), preferred_element_type=F32)


def mul_t(left, right):
    return lax.dot_general(left, right, (((1,), (1,)), ((), ())), preferred_element_type=F32)


def cos_sin_turn(fraction):
    half = (fraction - jnp.where(fraction >= 0.5, 1.0, 0.0)) * math.pi
    sq = half * half
    s = 1.0 / 6227020800.0
    for term in (-1.0 / 39916800.0, 1.0 / 362880.0, -1.0 / 5040.0, 1.0 / 120.0, -1.0 / 6.0, 1.0):
        s = s * sq + term
    s = s * half
    c = -1.0 / 87178291200.0
    for term in (
        1.0 / 479001600.0,
        -1.0 / 3628800.0,
        1.0 / 40320.0,
        -1.0 / 720.0,
        1.0 / 24.0,
        -0.5,
        1.0,
    ):
        c = c * sq + term
    return 1.0 - 2.0 * s * s, 2.0 * s * c


def log_bessel(power):
    edge = 3.75 * 3.75
    t = jnp.minimum(power, edge) * (1.0 / edge)
    small = jnp.full_like(t, 0.0045813)
    for term in (0.0360768, 0.2659732, 1.2067492, 3.0899424, 3.5156229, 1.0):
        small = small * t + term
    above = jnp.maximum(power, edge)
    inverse = lax.rsqrt(above)
    x = above * inverse
    q = 3.75 * inverse
    large = jnp.full_like(t, 0.00392377)
    for term in (
        -0.01647633,
        0.02635537,
        -0.02057706,
        0.00916281,
        -0.00157565,
        0.00225319,
        0.01328592,
        0.39894228,
    ):
        large = large * q + term
    is_small = power < edge
    return jnp.where(is_small, 0.0, x) + jnp.log(
        jnp.where(is_small, small, large * lax.rsqrt(x))
    )


def frame(ref, begin, count):
    return jnp.concatenate([ref[pl.ds(begin, count, 2), :], ref[pl.ds(begin + 1, count, 2), :]], axis=1)


def turning(cos, sin):
    return jnp.concatenate(
        [jnp.concatenate([cos, -sin], axis=1), jnp.concatenate([sin, cos], axis=1)], axis=0
    )


def thrice(high, low):
    return jnp.concatenate([high, low, high], axis=1)


def kernel(
    len_hbm, weight_hbm, mass_hbm, valid_hbm, strain_hbm, asd_hbm, tmpl_hbm, base_hbm, last_hbm, twist_hbm, pick_hbm,
    mine_log, mine_chirp, mine_delay, other_log, other_chirp, other_delay, log_prior,
    len_ref, weight_ref, mass_ref, valid_ref,
    strain, asd, tmpl, base, last, twist, pick,
    gated, halo, filt, corr, send, recv, trait, traits, prior, priors, zsend, zrecv,
    in_sem, halo_sem, send_sem, recv_sem, trait_send, trait_recv, prior_sem, zsend_sem, zrecv_sem,
):
    seg, bank = lax.axis_index("seg"), lax.axis_index("bank")
    seg_count = lax.axis_size("seg")
    y, z, core = bank // 4, bank // 2 % 2, bank % 2
    rank = y * 2 + core

    def bank_of(rank_, z_):
        return rank_ // 2 * 4 + z_ * 2 + rank_ % 2

    pairs = (
        (valid_hbm, valid_ref),
        (strain_hbm.at[256:384], strain.at[256:384]),
        (strain_hbm.at[0:256], strain.at[0:256]),
        (base_hbm, base),
        (len_hbm, len_ref),
        (weight_hbm, weight_ref),
        (mass_hbm, mass_ref),
        (pick_hbm, pick),
        (tmpl_hbm, tmpl),
        (asd_hbm, asd),
        (twist_hbm, twist),
        (last_hbm, last),
    )
    loads = [pltpu.make_async_copy(source, target, in_sem.at[i]) for i, (source, target) in enumerate(pairs)]
    loads[0].start()
    loads[1].start()

    barrier = pltpu.get_barrier_semaphore()

    @pl.when(seg > 0)
    def _():
        pl.semaphore_signal(barrier, inc=1, device_id=(seg - 1, bank), device_id_type=MESH)

    peers = [(seg, bank_of((rank + o) % GROUP, z)) for o in range(1, GROUP)]
    opposite = (seg, bank_of(rank, 1 - z))
    for peer in [opposite] + peers:
        pl.semaphore_signal(barrier, inc=1, device_id=peer, device_id_type=MESH)
    for load in loads[2:]:
        load.start()

    def gate(begin, end):
        for i in range(begin, end):
            gated[8 * i : 8 * i + 8, :] = strain[8 * i : 8 * i + 8, :] * valid_ref[i].astype(F32)

    loads[0].wait()
    loads[1].wait()
    gate(32, 48)

    pl.semaphore_wait(barrier, GROUP + 1 - (seg + 1) // seg_count)

    def halo_copy():
        return pltpu.make_async_remote_copy(
            src_ref=gated.at[256:384], dst_ref=halo, send_sem=halo_sem.at[0], recv_sem=halo_sem.at[1],
            device_id=(seg + 1, bank), device_id_type=MESH,
        )

    @pl.when(seg < seg_count - 1)
    def _():
        halo_copy().start()

    @pl.when(seg == 0)
    def _():
        halo[...] = jnp.zeros((128, 128), F32)

    for i in range(4, 7):
        loads[i].wait()
    row = lax.broadcasted_iota(jnp.int32, (8, 128), 0)
    facts = (
        weight_ref[0] + weight_ref[1],
        mass_ref[0],
        mass_ref[1],
        len_ref[0].astype(F32) * (1.0 / RATE),
        len_ref[1].astype(F32) * (1.0 / RATE),
    )
    tile = jnp.zeros((8, 128), F32)
    for i, fact in enumerate(facts):
        tile = jnp.where(row == i, fact, tile)
    trait[...] = tile
    trait_copies = [
        pltpu.make_async_remote_copy(
            src_ref=trait, dst_ref=traits.at[o], send_sem=trait_send.at[o], recv_sem=trait_recv.at[o],
            device_id=peers[o - 1], device_id_type=MESH,
        )
        for o in range(1, GROUP)
    ]
    for copy in trait_copies:
        copy.start()

    loads[2].wait()
    gate(0, 32)
    high, low = split(frame(gated, 0, 192))
    loads[3].wait()
    blank = jnp.zeros((64, 256), BF16)
    first = thrice(base[0], base[1])
    part = mul(first, jnp.concatenate([blank, high, blank, high, blank, low], axis=0))

    loads[7].wait()
    loads[8].wait()
    deal = []
    for i in range(4):
        rows = slice(128 * i, 128 * i + 128)
        deal.append(mul(pick[...], jnp.concatenate([tmpl[0, rows], tmpl[1, rows]], axis=1)))
    loads[9].wait()
    level = frame(asd, 0, 128)
    for k in range(2):
        parts = [
            jnp.concatenate([d[64 * k + 32 * h : 64 * k + 32 * h + 32] for d in deal], axis=0) for h in range(2)
        ]
        tmpl_re = jnp.concatenate([p[:, :128] for p in parts], axis=1)
        tmpl_im = jnp.concatenate([p[:, 128:] for p in parts], axis=1)
        sigma = jnp.sum(level * level * (tmpl_re * tmpl_re + tmpl_im * tmpl_im), keepdims=True)
        start = OVER - len_ref[k]
        index = lax.broadcasted_iota(jnp.int32, (128, 128), 0) * start % 256
        long_cos, long_sin = cos_sin_turn(index.astype(F32) * (1.0 / 256))
        index = lax.broadcasted_iota(jnp.int32, (1, 256), 1) * start % NFFT
        short_cos, short_sin = cos_sin_turn(index.astype(F32) * (1.0 / NFFT))
        long_cos = jnp.concatenate([long_cos, long_cos], axis=1)
        long_sin = jnp.concatenate([long_sin, long_sin], axis=1)
        turn_re = long_cos * short_cos - long_sin * short_sin
        turn_im = long_cos * short_sin + long_sin * short_cos
        scale = level * (lax.rsqrt(sigma) * (1.0 / math.sqrt(NFFT)))
        filt[k, 0] = (tmpl_re * turn_re + tmpl_im * turn_im) * scale
        filt[k, 1] = (tmpl_re * turn_im - tmpl_im * turn_re) * scale
    loads[10].wait()
    loads[11].wait()

    @pl.when(seg > 0)
    def _():
        halo_copy().wait_recv()

    high, low = split(frame(halo, 0, 64))
    part = part + mul(
        thrice(base[0, :, 0:128], base[1, :, 0:128]),
        jnp.concatenate([high, blank, high, blank, low, blank], axis=0),
    )
    twist_cos, twist_sin = twist[0], twist[1]

    turned = jnp.concatenate(
        [
            part[:256] * twist_cos - part[256:] * twist_sin,
            part[256:] * twist_cos + part[:256] * twist_sin,
        ],
        axis=1,
    )
    high, low = split(turned)
    second = [turning(base[i, 0:128], base[i, 256:384]) for i in range(2)]
    spec = mul_t(thrice(*second), jnp.concatenate([high, high, low], axis=1))
    spec_re, spec_im = spec[:128], spec[128:]
    third = thrice(*[turning(base[i, 0:256, 0:128], base[i, 256:512, 0:128]) for i in range(2)])
    fourth = thrice(*[turning(last[i, 0:192], last[i, 192:384]) for i in range(2)])
    for k in range(2):
        filt_re, filt_im = filt[k, 0], filt[k, 1]
        prod = jnp.concatenate(
            [spec_re * filt_re + spec_im * filt_im, spec_re * filt_im - spec_im * filt_re], axis=0
        )
        high, low = split(prod)
        inner = mul(third, jnp.concatenate([high, high, low], axis=0))
        turned = jnp.concatenate(
            [
                inner[:256] * twist_cos - inner[256:] * twist_sin,
                inner[:256] * twist_sin + inner[256:] * twist_cos,
            ],
            axis=1,
        )
        high, low = split(turned)
        corr[k] = mul_t(fourth, jnp.concatenate([high, high, low], axis=1))

    def score_copy(j, o):
        return pltpu.make_async_remote_copy(
            src_ref=send.at[j, (rank + o) % GROUP], dst_ref=recv.at[j, o],
            send_sem=send_sem.at[j, o], recv_sem=recv_sem.at[j, o],
            device_id=(seg, bank_of((rank + o) % GROUP, z)), device_id_type=MESH,
        )

    log_weight = [jnp.log(jnp.full((8, 256), weight_ref[k], F32)) for k in range(2)]
    for j in range(CHUNKS):
        for o in (4, 5, 3, 2, 6, 7, 1, 0):
            dest = (rank + o) % GROUP
            begin = pl.multiple_of(j * 64 + dest * 8, 8)
            for k in range(2):
                re = corr[k, pl.ds(begin, 8), :]
                im = corr[k, pl.ds(begin + 192, 8), :]
                send[j, dest, k] = log_bessel(re * re + im * im) + log_weight[k]
            if o:
                score_copy(j, o).start()

    for copy in trait_copies:
        copy.wait_recv()
    traits[0] = trait[...]
    weight_sum = traits[0, 0:1, :]
    for o in range(1, GROUP):
        weight_sum = weight_sum + traits[o, 0:1, :]
    prior[...] = jnp.broadcast_to(weight_sum, (8, 128))
    prior_copy = pltpu.make_async_remote_copy(
        src_ref=prior, dst_ref=priors, send_sem=prior_sem.at[0], recv_sem=prior_sem.at[1],
        device_id=opposite, device_id_type=MESH,
    )
    prior_copy.start()

    def z_copy(j):
        return pltpu.make_async_remote_copy(
            src_ref=zsend.at[j], dst_ref=zrecv.at[j], send_sem=zsend_sem.at[j], recv_sem=zrecv_sem.at[j],
            device_id=opposite, device_id_type=MESH,
        )

    for j in range(CHUNKS):
        for o in range(1, GROUP):
            score_copy(j, o).wait_recv()
        scores = [send[j, rank, k] for k in range(2)]
        for o in range(1, GROUP):
            scores += [recv[j, o, k] for k in range(2)]
        peak = functools.reduce(jnp.maximum, scores)
        total = chirp_sum = delay_sum = jnp.zeros((8, 256), F32)
        for i, score in enumerate(scores):
            o, k = divmod(i, 2)
            mass = jnp.exp(score - peak)
            total = total + mass
            chirp_sum = chirp_sum + mass * traits[o, 1 + k : 2 + k, 0:1]
            delay_sum = delay_sum + mass * traits[o, 3 + k : 4 + k, 0:1]
        inverse = 1.0 / total
        results = (peak + jnp.log(total), chirp_sum * inverse, delay_sum * inverse)
        for i, (value, out) in enumerate(zip(results, (mine_log, mine_chirp, mine_delay))):
            mine = jnp.where(z == 0, value[:4], value[4:])
            other = jnp.where(z == 0, value[4:], value[:4])
            for h in range(2):
                lanes = slice(128 * h, 128 * h + 128)
                out[pl.ds(8 * j + h, 4, 2), :] = mine[:, lanes]
                zsend[j, pl.ds(8 * i + h, 4, 2), :] = other[:, lanes]
        z_copy(j).start()

    prior_copy.wait_recv()
    level = jnp.log(prior[...] + priors[...])
    for j in range(CHUNKS):
        log_prior[8 * j : 8 * j + 8] = level

    @pl.when(seg < seg_count - 1)
    def _():
        halo_copy().wait_send()

    for copy in trait_copies + [prior_copy]:
        copy.wait_send()
    for j in range(CHUNKS):
        for o in range(1, GROUP):
            score_copy(j, o).wait_send()
    for j in range(CHUNKS):
        z_copy(j).wait_send()
    for j in range(CHUNKS):
        z_copy(j).wait_recv()
        for i, out in enumerate((other_log, other_chirp, other_delay)):
            out[8 * j : 8 * j + 8] = zrecv[j, 8 * i : 8 * i + 8]


def local(strain, inv_asd, templates, tmpl_len, weights, chirp_mass, valid):
    base, last, twist, pick = tables()
    dealt = templates.reshape(2, 2, 256, 128).transpose(0, 2, 1, 3).reshape(2, 512, 128)
    anywhere = pl.BlockSpec(memory_space=pl.ANY)
    held = pl.BlockSpec(memory_space=pltpu.VMEM)
    dma = pltpu.SemaphoreType.DMA
    mine_log, mine_chirp, mine_delay, other_log, other_chirp, other_delay, log_prior = pl.pallas_call(
        kernel,
        out_shape=(pltpu.VMEM((24, 128), F32),) * 7,
        in_specs=[anywhere] * 11,
        out_specs=(held,) * 7,
        scratch_shapes=[
            pltpu.SMEM((2,), jnp.int32),
            pltpu.SMEM((2,), F32),
            pltpu.SMEM((2,), F32),
            pltpu.SMEM((48,), jnp.int32),
            pltpu.VMEM((384, 128), F32),
            pltpu.VMEM((256, 128), F32),
            pltpu.VMEM((2, 512, 128), BF16),
            pltpu.VMEM(base.shape, BF16),
            pltpu.VMEM(last.shape, BF16),
            pltpu.VMEM(twist.shape, F32),
            pltpu.VMEM(pick.shape, BF16),
            pltpu.VMEM((384, 128), F32),
            pltpu.VMEM((128, 128), F32),
            pltpu.VMEM((2, 2, 128, 256), F32),
            pltpu.VMEM((2, 384, 256), F32),
            pltpu.VMEM((CHUNKS, GROUP, 2, 8, 256), F32),
            pltpu.VMEM((CHUNKS, GROUP, 2, 8, 256), F32),
            pltpu.VMEM((8, 128), F32),
            pltpu.VMEM((GROUP, 8, 128), F32),
            pltpu.VMEM((8, 128), F32),
            pltpu.VMEM((8, 128), F32),
            pltpu.VMEM((CHUNKS, 24, 128), F32),
            pltpu.VMEM((CHUNKS, 24, 128), F32),
            dma((12,)),
            dma((2,)),
            dma((CHUNKS, GROUP)),
            dma((CHUNKS, GROUP)),
            dma((GROUP,)),
            dma((GROUP,)),
            dma((2,)),
            dma((CHUNKS,)),
            dma((CHUNKS,)),
        ],
        compiler_params=pltpu.CompilerParams(
            collective_id=0, has_side_effects=True, vmem_limit_bytes=56 * 1024 * 1024
        ),
    )(
        tmpl_len, weights, chirp_mass, valid,
        strain.reshape(384, 128), inv_asd.reshape(256, 128), dealt, base, last, twist, pick,
    )
    peak = jnp.maximum(mine_log, other_log)
    mass_a, mass_b = jnp.exp(mine_log - peak), jnp.exp(other_log - peak)
    total = mass_a + mass_b
    outs = (
        peak + jnp.log(total) - log_prior,
        (mass_a * mine_chirp + mass_b * other_chirp) / total,
        (mass_a * mine_delay + mass_b * other_delay) / total,
    )
    return tuple(out.reshape(3072) for out in outs)


def solution(mesh):
    placed = (P("seg"), P(), P(None, "bank", None), P("bank"), P("bank"), P("bank"), P("seg"))
    return jax.shard_map(
        local,
        mesh=mesh,
        in_specs=placed,
        out_specs=(P(("seg", "bank")), P(("seg", "bank")), P(("seg", "bank"))),
        check_vma=False,
    )
```

```python
import functools
import math

import jax
import jax.numpy as jnp
import ml_dtypes
import numpy as np
from jax import lax
from jax.experimental import pallas as pl
from jax.experimental.pallas import tpu as pltpu
from jax.sharding import PartitionSpec as P

NFFT = 65536
OVER = 16384
RATE = 4096
HOP = 49152
F32, BF16 = jnp.float32, jnp.bfloat16
MESH = pl.DeviceIdType.MESH
HALVES = 2
GROUP = 8


def halves(table):
    high = table.astype(ml_dtypes.bfloat16)
    low = (table - high.astype(np.float64)).astype(ml_dtypes.bfloat16)
    return high, low


@functools.cache
def tables():
    turn = np.outer(np.arange(256), np.arange(256)) % 256 * (2 * np.pi / 256)
    base = np.stack(halves(np.concatenate([np.cos(turn), np.sin(turn)])))
    last = []
    for z in range(2):
        order = []
        for half in (1 - z, z):
            begins = [48 * y + 24 * half + 12 * core for y in range(4) for core in range(2)]
            order += [t + i for t in begins for i in range(8)] + [t + i for t in begins for i in range(8, 12)]
        last.append(halves(np.concatenate([np.cos(turn)[order], np.sin(turn)[order]])))
    last = np.array(last)
    twist = np.outer(np.arange(256), np.arange(256)) * (2 * np.pi / NFFT)
    twist = np.stack([np.cos(twist), np.sin(twist)]).astype(np.float32)
    pick = np.zeros((128, 128), ml_dtypes.bfloat16)
    for k in range(2):
        for h in range(2):
            for a in range(32):
                pick[k * 64 + h * 32 + a, (2 * a + h) * 2 + k] = 1
    return base, last, twist, pick


def split(value):
    high = value.astype(BF16)
    return high, (value - high.astype(F32)).astype(BF16)


def mul(left, right):
    return lax.dot_general(left, right, (((1,), (0,)), ((), ())), preferred_element_type=F32)


def mul_t(left, right):
    return lax.dot_general(left, right, (((1,), (1,)), ((), ())), preferred_element_type=F32)


def cos_sin_turn(fraction):
    half = (fraction - jnp.where(fraction >= 0.5, 1.0, 0.0)) * math.pi
    sq = half * half
    s = 1.0 / 6227020800.0
    for term in (-1.0 / 39916800.0, 1.0 / 362880.0, -1.0 / 5040.0, 1.0 / 120.0, -1.0 / 6.0, 1.0):
        s = s * sq + term
    s = s * half
    c = -1.0 / 87178291200.0
    for term in (
        1.0 / 479001600.0,
        -1.0 / 3628800.0,
        1.0 / 40320.0,
        -1.0 / 720.0,
        1.0 / 24.0,
        -0.5,
        1.0,
    ):
        c = c * sq + term
    return 1.0 - 2.0 * s * s, 2.0 * s * c


def log_bessel(power):
    edge = 3.75 * 3.75
    t = jnp.minimum(power, edge) * (1.0 / edge)
    small = jnp.full_like(t, 0.0045813)
    for term in (0.0360768, 0.2659732, 1.2067492, 3.0899424, 3.5156229, 1.0):
        small = small * t + term
    above = jnp.maximum(power, edge)
    inverse = lax.rsqrt(above)
    x = above * inverse
    q = 3.75 * inverse
    large = jnp.full_like(t, 0.00392377)
    for term in (
        -0.01647633,
        0.02635537,
        -0.02057706,
        0.00916281,
        -0.00157565,
        0.00225319,
        0.01328592,
        0.39894228,
    ):
        large = large * q + term
    is_small = power < edge
    return jnp.where(is_small, 0.0, x) + jnp.log(
        jnp.where(is_small, small, large * lax.rsqrt(x))
    )


def frame(ref, begin, count):
    return jnp.concatenate([ref[pl.ds(begin, count, 2), :], ref[pl.ds(begin + 1, count, 2), :]], axis=1)


def turning(cos, sin):
    return jnp.concatenate(
        [jnp.concatenate([cos, -sin], axis=1), jnp.concatenate([sin, cos], axis=1)], axis=0
    )


def thrice(high, low):
    return jnp.concatenate([high, low, high], axis=1)


def prepare(
    len_hbm, weight_hbm, mass_hbm, valid_hbm, strain_hbm, asd_hbm, tmpl_hbm, base_hbm, last_hbm, twist_hbm, pick_hbm,
    part_out, filt, trait, base, last, twist,
    len_ref, weight_ref, mass_ref, valid_ref, strain, asd, tmpl, pick, gated, halo, in_sem, halo_sem,
):
    seg, bank = lax.axis_index("seg"), lax.axis_index("bank")
    seg_count = lax.axis_size("seg")
    barrier = pltpu.get_barrier_semaphore()

    @pl.when(seg > 0)
    def _():
        pl.semaphore_signal(barrier, inc=1, device_id=(seg - 1, bank), device_id_type=MESH)

    pairs = (
        (valid_hbm, valid_ref),
        (strain_hbm.at[256:384], strain.at[256:384]),
        (strain_hbm.at[0:256], strain.at[0:256]),
        (base_hbm, base),
        (len_hbm, len_ref),
        (weight_hbm, weight_ref),
        (mass_hbm, mass_ref),
        (pick_hbm, pick),
        (tmpl_hbm, tmpl),
        (asd_hbm, asd),
        (twist_hbm, twist),
        (last_hbm.at[bank // 2 % 2], last),
    )
    loads = [pltpu.make_async_copy(source, target, in_sem.at[i]) for i, (source, target) in enumerate(pairs)]
    loads[0].start()
    loads[1].start()
    for load in loads[2:]:
        load.start()

    def gate(begin, end):
        for i in range(begin, end):
            gated[8 * i : 8 * i + 8, :] = strain[8 * i : 8 * i + 8, :] * valid_ref[i].astype(F32)

    loads[0].wait()
    loads[1].wait()
    gate(32, 48)

    def halo_copy():
        return pltpu.make_async_remote_copy(
            src_ref=gated.at[256:384], dst_ref=halo, send_sem=halo_sem.at[0], recv_sem=halo_sem.at[1],
            device_id=(seg + 1, bank), device_id_type=MESH,
        )

    @pl.when(seg < seg_count - 1)
    def _():
        pl.semaphore_wait(barrier, 1)
        halo_copy().start()

    @pl.when(seg == 0)
    def _():
        halo[...] = jnp.zeros((128, 128), F32)

    for i in range(4, 7):
        loads[i].wait()
    row = lax.broadcasted_iota(jnp.int32, (8, 128), 0)
    facts = (
        weight_ref[0] + weight_ref[1],
        mass_ref[0],
        mass_ref[1],
        len_ref[0].astype(F32) * (1.0 / RATE),
        len_ref[1].astype(F32) * (1.0 / RATE),
        weight_ref[0],
        weight_ref[1],
    )
    tile = jnp.zeros((8, 128), F32)
    for i, fact in enumerate(facts):
        tile = jnp.where(row == i, fact, tile)
    trait[...] = tile

    loads[2].wait()
    gate(0, 32)
    high, low = split(frame(gated, 0, 192))
    loads[3].wait()
    blank = jnp.zeros((64, 256), BF16)
    first = thrice(base[0], base[1])
    part = mul(first, jnp.concatenate([blank, high, blank, high, blank, low], axis=0))

    loads[7].wait()
    loads[8].wait()
    deal = []
    for i in range(4):
        rows = slice(128 * i, 128 * i + 128)
        deal.append(mul(pick[...], jnp.concatenate([tmpl[0, rows], tmpl[1, rows]], axis=1)))
    loads[9].wait()
    level = frame(asd, 0, 128)
    for k in range(2):
        parts = [
            jnp.concatenate([d[64 * k + 32 * h : 64 * k + 32 * h + 32] for d in deal], axis=0) for h in range(2)
        ]
        tmpl_re = jnp.concatenate([p[:, :128] for p in parts], axis=1)
        tmpl_im = jnp.concatenate([p[:, 128:] for p in parts], axis=1)
        sigma = jnp.sum(level * level * (tmpl_re * tmpl_re + tmpl_im * tmpl_im), keepdims=True)
        start = OVER - len_ref[k]
        index = lax.broadcasted_iota(jnp.int32, (128, 128), 0) * start % 256
        long_cos, long_sin = cos_sin_turn(index.astype(F32) * (1.0 / 256))
        index = lax.broadcasted_iota(jnp.int32, (1, 256), 1) * start % NFFT
        short_cos, short_sin = cos_sin_turn(index.astype(F32) * (1.0 / NFFT))
        long_cos = jnp.concatenate([long_cos, long_cos], axis=1)
        long_sin = jnp.concatenate([long_sin, long_sin], axis=1)
        turn_re = long_cos * short_cos - long_sin * short_sin
        turn_im = long_cos * short_sin + long_sin * short_cos
        scale = level * (lax.rsqrt(sigma) * (1.0 / math.sqrt(NFFT)))
        filt[k, 0] = (tmpl_re * turn_re + tmpl_im * turn_im) * scale
        filt[k, 1] = (tmpl_re * turn_im - tmpl_im * turn_re) * scale
    loads[10].wait()
    loads[11].wait()

    @pl.when(seg > 0)
    def _():
        halo_copy().wait_recv()

    high, low = split(frame(halo, 0, 64))
    part_out[...] = part + mul(
        thrice(base[0, :, 0:128], base[1, :, 0:128]),
        jnp.concatenate([high, blank, high, blank, low, blank], axis=0),
    )

    @pl.when(seg < seg_count - 1)
    def _():
        halo_copy().wait_send()


def match(
    part, filt, trait, base, last, twist,
    mine_log, mine_chirp, mine_delay, other_log, other_chirp, other_delay, log_prior,
    send, recv, traits, packet, arrived, send_sem, recv_sem, trait_send, trait_recv, z_sem,
):
    seg, bank = lax.axis_index("seg"), lax.axis_index("bank")
    y, z, core = bank // 4, bank // 2 % 2, bank % 2
    rank = y * 2 + core

    def bank_of(rank_, z_):
        return rank_ // 2 * 4 + z_ * 2 + rank_ % 2

    barrier = pltpu.get_barrier_semaphore()
    peers = [(seg, bank_of((rank + o) % GROUP, z)) for o in range(1, GROUP)]
    opposite = (seg, bank_of(rank, 1 - z))
    for peer in [opposite] + peers:
        pl.semaphore_signal(barrier, inc=1, device_id=peer, device_id_type=MESH)
    twist_cos, twist_sin = twist[0], twist[1]

    turned = jnp.concatenate(
        [
            part[0:256] * twist_cos - part[256:512] * twist_sin,
            part[256:512] * twist_cos + part[0:256] * twist_sin,
        ],
        axis=1,
    )
    high, low = split(turned)
    second = [turning(base[i, 0:128], base[i, 256:384]) for i in range(2)]
    spec = mul_t(thrice(*second), jnp.concatenate([high, high, low], axis=1))
    spec_re, spec_im = spec[:128], spec[128:]
    third = thrice(*[turning(base[i, 0:256, 0:128], base[i, 256:512, 0:128]) for i in range(2)])
    fourth = thrice(*[turning(last[i, 0:192], last[i, 192:384]) for i in range(2)])
    weights = []
    for k in range(2):
        filt_re, filt_im = filt[k, 0], filt[k, 1]
        prod = jnp.concatenate(
            [spec_re * filt_re + spec_im * filt_im, spec_re * filt_im - spec_im * filt_re], axis=0
        )
        high, low = split(prod)
        inner = mul(third, jnp.concatenate([high, high, low], axis=0))
        turned = jnp.concatenate(
            [
                inner[:256] * twist_cos - inner[256:] * twist_sin,
                inner[:256] * twist_sin + inner[256:] * twist_cos,
            ],
            axis=1,
        )
        high, low = split(turned)
        weights.append(jnp.concatenate([high, high, low], axis=1))

    def score_copy(j, o):
        return pltpu.make_async_remote_copy(
            src_ref=send.at[j, (rank + o) % GROUP], dst_ref=recv.at[j, o],
            send_sem=send_sem.at[j, o], recv_sem=recv_sem.at[j, o],
            device_id=peers[o - 1], device_id_type=MESH,
        )

    trait_copies = [
        pltpu.make_async_remote_copy(
            src_ref=trait, dst_ref=traits.at[o], send_sem=trait_send.at[o], recv_sem=trait_recv.at[o],
            device_id=peers[o - 1], device_id_type=MESH,
        )
        for o in range(1, GROUP)
    ]
    log_weight = [jnp.log(jnp.broadcast_to(trait[5 + k : 6 + k, 0:1], (8, 256))) for k in range(2)]
    for j in range(HALVES):
        fourth = thrice(
            *[turning(last[i, 96 * j : 96 * j + 96], last[i, 96 * j + 192 : 96 * j + 288]) for i in range(2)]
        )
        for k in range(2):
            corr = mul_t(fourth, weights[k])

            def score(p):
                re, im = corr[p : p + 8], corr[p + 96 : p + 104]
                return log_bessel(re * re + im * im) + log_weight[k]

            for block in range(GROUP):
                send[j, block, 8 * k : 8 * k + 8] = score(8 * block)
            for block in range(0, GROUP, 2):
                both = score(64 + 4 * block)
                send[j, block, 16 + 4 * k : 20 + 4 * k] = both[:4]
                send[j, block + 1, 16 + 4 * k : 20 + 4 * k] = both[4:]
        if j == 0:
            pl.semaphore_wait(barrier, GROUP)
        for o in (4, 5, 3, 2, 6, 7, 1):
            score_copy(j, o).start()
        if j == 0:
            for copy in trait_copies:
                copy.start()

    for copy in trait_copies:
        copy.wait_recv()
    traits[0] = trait[...]
    weight_sum = traits[0, 0:1, :]
    for o in range(1, GROUP):
        weight_sum = weight_sum + traits[o, 0:1, :]
    packet[72:80] = jnp.broadcast_to(weight_sum, (8, 128))

    z_copy = pltpu.make_async_remote_copy(
        src_ref=packet, dst_ref=arrived, send_sem=z_sem.at[0], recv_sem=z_sem.at[1],
        device_id=opposite, device_id_type=MESH,
    )
    is_first = lax.broadcasted_iota(jnp.int32, (8, 256), 0) < 4
    for j in range(HALVES):
        for o in range(1, GROUP):
            score_copy(j, o).wait_recv()

        def arrivals(begin):
            return [send[j, rank, begin : begin + 8]] + [recv[j, o, begin : begin + 8] for o in range(1, GROUP)]

        def fact(o, i):
            return traits[o, i : i + 1, 0:1]

        scores = [arrivals(0), arrivals(8)]
        peak = functools.reduce(jnp.maximum, scores[0] + scores[1])
        total = chirp_sum = delay_sum = jnp.zeros((8, 256), F32)
        for o in range(GROUP):
            for k in range(2):
                mass = jnp.exp(scores[k][o] - peak)
                total = total + mass
                chirp_sum = chirp_sum + mass * fact(o, 1 + k)
                delay_sum = delay_sum + mass * fact(o, 3 + k)
        inverse = 1.0 / total
        upper = (peak + jnp.log(total), chirp_sum * inverse, delay_sum * inverse)

        scores = arrivals(16)
        peak = functools.reduce(jnp.maximum, scores)
        peak = jnp.maximum(peak[:4], peak[4:])
        peak_twice = jnp.concatenate([peak, peak], axis=0)
        total = chirp_sum = delay_sum = jnp.zeros((8, 256), F32)
        for o in range(GROUP):
            mass = jnp.exp(scores[o] - peak_twice)
            total = total + mass
            chirp_sum = chirp_sum + mass * jnp.where(is_first, fact(o, 1), fact(o, 2))
            delay_sum = delay_sum + mass * jnp.where(is_first, fact(o, 3), fact(o, 4))
        total, chirp_sum, delay_sum = [v[:4] + v[4:] for v in (total, chirp_sum, delay_sum)]
        inverse = 1.0 / total
        lower = (peak + jnp.log(total), chirp_sum * inverse, delay_sum * inverse)

        for i, out in enumerate((mine_log, mine_chirp, mine_delay)):
            for h in range(2):
                lanes = slice(128 * h, 128 * h + 128)
                if j == 0:
                    packet[pl.ds(24 * i + h, 8, 2), :] = upper[i][:, lanes]
                    packet[pl.ds(24 * i + 16 + h, 4, 2), :] = lower[i][:, lanes]
                else:
                    out[pl.ds(h, 8, 2), :] = upper[i][:, lanes]
                    out[pl.ds(16 + h, 4, 2), :] = lower[i][:, lanes]
        if j == 0:
            z_copy.start()

    for copy in trait_copies:
        copy.wait_send()
    for j in range(HALVES):
        for o in range(1, GROUP):
            score_copy(j, o).wait_send()
    z_copy.wait()
    for i, out in enumerate((other_log, other_chirp, other_delay)):
        out[...] = arrived[24 * i : 24 * i + 24]
    level = jnp.log(packet[72:80] + arrived[72:80])
    for i in range(3):
        log_prior[8 * i : 8 * i + 8] = level


def local(strain, inv_asd, templates, tmpl_len, weights, chirp_mass, valid):
    base, last, twist, pick = tables()
    dealt = templates.reshape(2, 2, 256, 128).transpose(0, 2, 1, 3).reshape(2, 512, 128)
    anywhere = pl.BlockSpec(memory_space=pl.ANY)
    held = pl.BlockSpec(memory_space=pltpu.VMEM)
    dma = pltpu.SemaphoreType.DMA
    ready = pl.pallas_call(
        prepare,
        out_shape=(
            pltpu.VMEM((512, 256), F32),
            pltpu.VMEM((2, 2, 128, 256), F32),
            pltpu.VMEM((8, 128), F32),
            pltpu.VMEM(base.shape, BF16),
            pltpu.VMEM(last.shape[1:], BF16),
            pltpu.VMEM(twist.shape, F32),
        ),
        in_specs=[anywhere] * 11,
        out_specs=(held,) * 6,
        scratch_shapes=[
            pltpu.SMEM((2,), jnp.int32),
            pltpu.SMEM((2,), F32),
            pltpu.SMEM((2,), F32),
            pltpu.SMEM((48,), jnp.int32),
            pltpu.VMEM((384, 128), F32),
            pltpu.VMEM((256, 128), F32),
            pltpu.VMEM((2, 512, 128), BF16),
            pltpu.VMEM(pick.shape, BF16),
            pltpu.VMEM((384, 128), F32),
            pltpu.VMEM((128, 128), F32),
            dma((12,)),
            dma((2,)),
        ],
        compiler_params=pltpu.CompilerParams(
            collective_id=0, has_side_effects=True, vmem_limit_bytes=56 * 1024 * 1024
        ),
    )(
        tmpl_len, weights, chirp_mass, valid,
        strain.reshape(384, 128), inv_asd.reshape(256, 128), dealt, base, last, twist, pick,
    )
    mine_log, mine_chirp, mine_delay, other_log, other_chirp, other_delay, log_prior = pl.pallas_call(
        match,
        out_shape=(pltpu.VMEM((24, 128), F32),) * 7,
        in_specs=[held] * 6,
        out_specs=(held,) * 7,
        scratch_shapes=[
            pltpu.VMEM((HALVES, GROUP, 24, 256), F32),
            pltpu.VMEM((HALVES, GROUP, 24, 256), F32),
            pltpu.VMEM((GROUP, 8, 128), F32),
            pltpu.VMEM((80, 128), F32),
            pltpu.VMEM((80, 128), F32),
            dma((HALVES, GROUP)),
            dma((HALVES, GROUP)),
            dma((GROUP,)),
            dma((GROUP,)),
            dma((2,)),
        ],
        compiler_params=pltpu.CompilerParams(
            collective_id=1, has_side_effects=True, vmem_limit_bytes=56 * 1024 * 1024
        ),
    )(*[pltpu.with_memory_space_constraint(array, pltpu.VMEM) for array in ready])
    peak = jnp.maximum(mine_log, other_log)
    mass_a, mass_b = jnp.exp(mine_log - peak), jnp.exp(other_log - peak)
    total = mass_a + mass_b
    outs = (
        peak + jnp.log(total) - log_prior,
        (mass_a * mine_chirp + mass_b * other_chirp) / total,
        (mass_a * mine_delay + mass_b * other_delay) / total,
    )
    return tuple(out.reshape(3072) for out in outs)


def solution(mesh):
    placed = (P("seg"), P(), P(None, "bank", None), P("bank"), P("bank"), P("bank"), P("seg"))
    return jax.shard_map(
        local,
        mesh=mesh,
        in_specs=placed,
        out_specs=(P(("seg", "bank")), P(("seg", "bank")), P(("seg", "bank"))),
        check_vma=False,
    )
```

```python
import functools
import math

import jax
import jax.numpy as jnp
import ml_dtypes
import numpy as np
from jax import lax
from jax.experimental import pallas as pl
from jax.experimental.pallas import tpu as pltpu
from jax.sharding import PartitionSpec as P

NFFT = 65536
OVER = 16384
RATE = 4096
HOP = 49152
F32, BF16 = jnp.float32, jnp.bfloat16
MESH = pl.DeviceIdType.MESH
HALVES = 2
GROUP = 8


def halves(table):
    high = table.astype(ml_dtypes.bfloat16)
    low = (table - high.astype(np.float64)).astype(ml_dtypes.bfloat16)
    return high, low


@functools.cache
def tables():
    turn = np.outer(np.arange(256), np.arange(256)) % 256 * (2 * np.pi / 256)
    base = np.stack(halves(np.concatenate([np.cos(turn), np.sin(turn)])))
    last = []
    for z in range(2):
        order = []
        for half in (1 - z, z):
            begins = [48 * y + 24 * half + 12 * core for y in range(4) for core in range(2)]
            order += [t + i for t in begins for i in range(8)] + [t + i for t in begins for i in range(8, 12)]
        last.append(halves(np.concatenate([np.cos(turn)[order], np.sin(turn)[order]])))
    last = np.array(last)
    twist = np.outer(np.arange(256), np.arange(256)) * (2 * np.pi / NFFT)
    twist = np.stack([np.cos(twist), np.sin(twist)]).astype(np.float32)
    pick = np.zeros((128, 128), ml_dtypes.bfloat16)
    for k in range(2):
        for h in range(2):
            for a in range(32):
                pick[k * 64 + h * 32 + a, (2 * a + h) * 2 + k] = 1
    return base, last, twist, pick


def split(value):
    high = value.astype(BF16)
    return high, (value - high.astype(F32)).astype(BF16)


def mul(left, right):
    return lax.dot_general(left, right, (((1,), (0,)), ((), ())), preferred_element_type=F32)


def mul_t(left, right):
    return lax.dot_general(left, right, (((1,), (1,)), ((), ())), preferred_element_type=F32)


def cos_sin_turn(fraction):
    half = (fraction - jnp.where(fraction >= 0.5, 1.0, 0.0)) * math.pi
    sq = half * half
    s = 1.0 / 6227020800.0
    for term in (-1.0 / 39916800.0, 1.0 / 362880.0, -1.0 / 5040.0, 1.0 / 120.0, -1.0 / 6.0, 1.0):
        s = s * sq + term
    s = s * half
    c = -1.0 / 87178291200.0
    for term in (
        1.0 / 479001600.0,
        -1.0 / 3628800.0,
        1.0 / 40320.0,
        -1.0 / 720.0,
        1.0 / 24.0,
        -0.5,
        1.0,
    ):
        c = c * sq + term
    return 1.0 - 2.0 * s * s, 2.0 * s * c


def log_bessel(power):
    edge = 3.75 * 3.75
    t = jnp.minimum(power, edge) * (1.0 / edge)
    small = jnp.full_like(t, 0.0045813)
    for term in (0.0360768, 0.2659732, 1.2067492, 3.0899424, 3.5156229, 1.0):
        small = small * t + term
    above = jnp.maximum(power, edge)
    inverse = lax.rsqrt(above)
    x = above * inverse
    q = 3.75 * inverse
    large = jnp.full_like(t, 0.00392377)
    for term in (
        -0.01647633,
        0.02635537,
        -0.02057706,
        0.00916281,
        -0.00157565,
        0.00225319,
        0.01328592,
        0.39894228,
    ):
        large = large * q + term
    is_small = power < edge
    return jnp.where(is_small, 0.0, x) + jnp.log(
        jnp.where(is_small, small, large * lax.rsqrt(x))
    )


def frame(ref, begin, count):
    return jnp.concatenate([ref[pl.ds(begin, count, 2), :], ref[pl.ds(begin + 1, count, 2), :]], axis=1)


def turning(cos, sin):
    return jnp.concatenate(
        [jnp.concatenate([cos, -sin], axis=1), jnp.concatenate([sin, cos], axis=1)], axis=0
    )


def thrice(high, low):
    return jnp.concatenate([high, low, high], axis=1)


def prepare(
    len_hbm, weight_hbm, mass_hbm, valid_hbm, strain_hbm, asd_hbm, tmpl_hbm, base_hbm, last_hbm, twist_hbm, pick_hbm,
    part_out, filt, trait, base, last, twist,
    len_ref, weight_ref, mass_ref, valid_ref, strain, asd, tmpl, pick, gated, halo, in_sem, halo_sem,
):
    seg, bank = lax.axis_index("seg"), lax.axis_index("bank")
    seg_count = lax.axis_size("seg")
    barrier = pltpu.get_barrier_semaphore()

    @pl.when(seg > 0)
    def _():
        pl.semaphore_signal(barrier, inc=1, device_id=(seg - 1, bank), device_id_type=MESH)

    pairs = (
        (valid_hbm, valid_ref),
        (strain_hbm.at[256:384], strain.at[256:384]),
        (strain_hbm.at[0:256], strain.at[0:256]),
        (base_hbm, base),
        (len_hbm, len_ref),
        (weight_hbm, weight_ref),
        (mass_hbm, mass_ref),
        (pick_hbm, pick),
        (tmpl_hbm, tmpl),
        (asd_hbm, asd),
        (twist_hbm, twist),
        (last_hbm.at[bank // 2 % 2], last),
    )
    loads = [pltpu.make_async_copy(source, target, in_sem.at[i]) for i, (source, target) in enumerate(pairs)]
    loads[0].start()
    loads[1].start()
    for load in loads[2:]:
        load.start()

    def gate(begin, end):
        for i in range(begin, end):
            gated[8 * i : 8 * i + 8, :] = strain[8 * i : 8 * i + 8, :] * valid_ref[i].astype(F32)

    loads[0].wait()
    loads[1].wait()
    gate(32, 48)

    def halo_copy():
        return pltpu.make_async_remote_copy(
            src_ref=gated.at[256:384], dst_ref=halo, send_sem=halo_sem.at[0], recv_sem=halo_sem.at[1],
            device_id=(seg + 1, bank), device_id_type=MESH,
        )

    @pl.when(seg < seg_count - 1)
    def _():
        pl.semaphore_wait(barrier, 1)
        halo_copy().start()

    @pl.when(seg == 0)
    def _():
        halo[...] = jnp.zeros((128, 128), F32)

    for i in range(4, 7):
        loads[i].wait()
    row = lax.broadcasted_iota(jnp.int32, (8, 128), 0)
    facts = (
        weight_ref[0] + weight_ref[1],
        mass_ref[0],
        mass_ref[1],
        len_ref[0].astype(F32) * (1.0 / RATE),
        len_ref[1].astype(F32) * (1.0 / RATE),
        weight_ref[0],
        weight_ref[1],
    )
    tile = jnp.zeros((8, 128), F32)
    for i, fact in enumerate(facts):
        tile = jnp.where(row == i, fact, tile)
    trait[...] = tile

    loads[2].wait()
    gate(0, 32)
    high, low = split(frame(gated, 0, 192))
    loads[3].wait()
    blank = jnp.zeros((64, 256), BF16)
    first = thrice(base[0], base[1])
    part = mul(first, jnp.concatenate([blank, high, blank, high, blank, low], axis=0))

    loads[7].wait()
    loads[8].wait()
    deal = []
    for i in range(4):
        rows = slice(128 * i, 128 * i + 128)
        deal.append(mul(pick[...], jnp.concatenate([tmpl[0, rows], tmpl[1, rows]], axis=1)))
    loads[9].wait()
    level = frame(asd, 0, 128)
    for k in range(2):
        parts = [
            jnp.concatenate([d[64 * k + 32 * h : 64 * k + 32 * h + 32] for d in deal], axis=0) for h in range(2)
        ]
        tmpl_re = jnp.concatenate([p[:, :128] for p in parts], axis=1)
        tmpl_im = jnp.concatenate([p[:, 128:] for p in parts], axis=1)
        sigma = jnp.sum(level * level * (tmpl_re * tmpl_re + tmpl_im * tmpl_im), keepdims=True)
        start = OVER - len_ref[k]
        index = lax.broadcasted_iota(jnp.int32, (128, 128), 0) * start % 256
        long_cos, long_sin = cos_sin_turn(index.astype(F32) * (1.0 / 256))
        index = lax.broadcasted_iota(jnp.int32, (1, 256), 1) * start % NFFT
        short_cos, short_sin = cos_sin_turn(index.astype(F32) * (1.0 / NFFT))
        long_cos = jnp.concatenate([long_cos, long_cos], axis=1)
        long_sin = jnp.concatenate([long_sin, long_sin], axis=1)
        turn_re = long_cos * short_cos - long_sin * short_sin
        turn_im = long_cos * short_sin + long_sin * short_cos
        scale = level * (lax.rsqrt(sigma) * (1.0 / math.sqrt(NFFT)))
        filt[k, 0] = (tmpl_re * turn_re + tmpl_im * turn_im) * scale
        filt[k, 1] = (tmpl_re * turn_im - tmpl_im * turn_re) * scale
    loads[10].wait()
    loads[11].wait()

    @pl.when(seg > 0)
    def _():
        halo_copy().wait_recv()

    high, low = split(frame(halo, 0, 64))
    part_out[...] = part + mul(
        thrice(base[0, :, 0:128], base[1, :, 0:128]),
        jnp.concatenate([high, blank, high, blank, low, blank], axis=0),
    )

    @pl.when(seg < seg_count - 1)
    def _():
        halo_copy().wait_send()


def match(
    part, filt, trait, base, last, twist,
    mine_log, mine_chirp, mine_delay, other_log, other_chirp, other_delay, log_prior,
    send, recv, traits, packet, arrived, send_sem, recv_sem, trait_send, trait_recv, z_sem,
):
    seg, bank = lax.axis_index("seg"), lax.axis_index("bank")
    y, z, core = bank // 4, bank // 2 % 2, bank % 2
    rank = y * 2 + core

    def bank_of(rank_, z_):
        return rank_ // 2 * 4 + z_ * 2 + rank_ % 2

    barrier = pltpu.get_barrier_semaphore()
    peers = [(seg, bank_of((rank + o) % GROUP, z)) for o in range(1, GROUP)]
    opposite = (seg, bank_of(rank, 1 - z))
    for peer in [opposite] + peers:
        pl.semaphore_signal(barrier, inc=1, device_id=peer, device_id_type=MESH)
    twist_cos, twist_sin = twist[0], twist[1]

    turned = jnp.concatenate(
        [
            part[0:256] * twist_cos - part[256:512] * twist_sin,
            part[256:512] * twist_cos + part[0:256] * twist_sin,
        ],
        axis=1,
    )
    high, low = split(turned)
    second = [turning(base[i, 0:128], base[i, 256:384]) for i in range(2)]
    spec = mul_t(jnp.concatenate(second, axis=0), high)
    spec = spec[:256] + spec[256:] + mul_t(second[0], low)
    spec_re, spec_im = spec[:128], spec[128:]
    third = thrice(*[turning(base[i, 0:256, 0:128], base[i, 256:512, 0:128]) for i in range(2)])
    fourth = thrice(*[turning(last[i, 0:192], last[i, 192:384]) for i in range(2)])
    weights = []
    for k in range(2):
        filt_re, filt_im = filt[k, 0], filt[k, 1]
        prod = jnp.concatenate(
            [spec_re * filt_re + spec_im * filt_im, spec_re * filt_im - spec_im * filt_re], axis=0
        )
        high, low = split(prod)
        inner = mul(third, jnp.concatenate([high, high, low], axis=0))
        turned = jnp.concatenate(
            [
                inner[:256] * twist_cos - inner[256:] * twist_sin,
                inner[:256] * twist_sin + inner[256:] * twist_cos,
            ],
            axis=1,
        )
        high, low = split(turned)
        weights.append((high, low))

    def score_copy(j, o):
        return pltpu.make_async_remote_copy(
            src_ref=send.at[j, (rank + o) % GROUP], dst_ref=recv.at[j, o],
            send_sem=send_sem.at[j, o], recv_sem=recv_sem.at[j, o],
            device_id=peers[o - 1], device_id_type=MESH,
        )

    trait_copies = [
        pltpu.make_async_remote_copy(
            src_ref=trait, dst_ref=traits.at[o], send_sem=trait_send.at[o], recv_sem=trait_recv.at[o],
            device_id=peers[o - 1], device_id_type=MESH,
        )
        for o in range(1, GROUP)
    ]
    log_weight = [jnp.log(jnp.broadcast_to(trait[5 + k : 6 + k, 0:1], (8, 256))) for k in range(2)]
    for j in range(HALVES):
        fourth = [turning(last[i, 96 * j : 96 * j + 96], last[i, 96 * j + 192 : 96 * j + 288]) for i in range(2)]
        stacked = jnp.concatenate(fourth, axis=0)
        for k in range(2):
            high, low = weights[k]
            corr = mul_t(stacked, high)
            corr = corr[:192] + corr[192:] + mul_t(fourth[0], low)

            def score(p):
                re, im = corr[p : p + 8], corr[p + 96 : p + 104]
                return log_bessel(re * re + im * im) + log_weight[k]

            for block in range(GROUP):
                send[j, block, 8 * k : 8 * k + 8] = score(8 * block)
            for block in range(0, GROUP, 2):
                both = score(64 + 4 * block)
                send[j, block, 16 + 4 * k : 20 + 4 * k] = both[:4]
                send[j, block + 1, 16 + 4 * k : 20 + 4 * k] = both[4:]
        if j == 0:
            pl.semaphore_wait(barrier, GROUP)
            for copy in trait_copies:
                copy.start()
            for o in (4, 5, 3, 2, 6, 7, 1):
                score_copy(0, o).start()

    for copy in trait_copies:
        copy.wait_recv()
    traits[0] = trait[...]
    weight_sum = traits[0, 0:1, :]
    for o in range(1, GROUP):
        weight_sum = weight_sum + traits[o, 0:1, :]
    packet[72:80] = jnp.broadcast_to(weight_sum, (8, 128))

    z_copy = pltpu.make_async_remote_copy(
        src_ref=packet, dst_ref=arrived, send_sem=z_sem.at[0], recv_sem=z_sem.at[1],
        device_id=opposite, device_id_type=MESH,
    )
    is_first = lax.broadcasted_iota(jnp.int32, (8, 256), 0) < 4
    for j in range(HALVES):
        for o in range(1, GROUP):
            score_copy(j, o).wait_recv()
        if j == 0:
            for o in (4, 5, 3, 2, 6, 7, 1):
                score_copy(1, o).start()

        def arrivals(begin):
            return [send[j, rank, begin : begin + 8]] + [recv[j, o, begin : begin + 8] for o in range(1, GROUP)]

        def fact(o, i):
            return traits[o, i : i + 1, 0:1]

        scores = [arrivals(0), arrivals(8)]
        peak = functools.reduce(jnp.maximum, scores[0] + scores[1])
        total = chirp_sum = delay_sum = jnp.zeros((8, 256), F32)
        for o in range(GROUP):
            for k in range(2):
                mass = jnp.exp(scores[k][o] - peak)
                total = total + mass
                chirp_sum = chirp_sum + mass * fact(o, 1 + k)
                delay_sum = delay_sum + mass * fact(o, 3 + k)
        inverse = 1.0 / total
        upper = (peak + jnp.log(total), chirp_sum * inverse, delay_sum * inverse)

        scores = arrivals(16)
        peak = functools.reduce(jnp.maximum, scores)
        peak = jnp.maximum(peak[:4], peak[4:])
        peak_twice = jnp.concatenate([peak, peak], axis=0)
        total = chirp_sum = delay_sum = jnp.zeros((8, 256), F32)
        for o in range(GROUP):
            mass = jnp.exp(scores[o] - peak_twice)
            total = total + mass
            chirp_sum = chirp_sum + mass * jnp.where(is_first, fact(o, 1), fact(o, 2))
            delay_sum = delay_sum + mass * jnp.where(is_first, fact(o, 3), fact(o, 4))
        total, chirp_sum, delay_sum = [v[:4] + v[4:] for v in (total, chirp_sum, delay_sum)]
        inverse = 1.0 / total
        lower = (peak + jnp.log(total), chirp_sum * inverse, delay_sum * inverse)

        for i, out in enumerate((mine_log, mine_chirp, mine_delay)):
            for h in range(2):
                lanes = slice(128 * h, 128 * h + 128)
                if j == 0:
                    packet[pl.ds(24 * i + h, 8, 2), :] = upper[i][:, lanes]
                    packet[pl.ds(24 * i + 16 + h, 4, 2), :] = lower[i][:, lanes]
                else:
                    out[pl.ds(h, 8, 2), :] = upper[i][:, lanes]
                    out[pl.ds(16 + h, 4, 2), :] = lower[i][:, lanes]
        if j == 0:
            z_copy.start()

    for copy in trait_copies:
        copy.wait_send()
    for j in range(HALVES):
        for o in range(1, GROUP):
            score_copy(j, o).wait_send()
    z_copy.wait()
    for i, out in enumerate((other_log, other_chirp, other_delay)):
        out[...] = arrived[24 * i : 24 * i + 24]
    level = jnp.log(packet[72:80] + arrived[72:80])
    for i in range(3):
        log_prior[8 * i : 8 * i + 8] = level


def local(strain, inv_asd, templates, tmpl_len, weights, chirp_mass, valid):
    base, last, twist, pick = tables()
    dealt = templates.reshape(2, 2, 256, 128).transpose(0, 2, 1, 3).reshape(2, 512, 128)
    anywhere = pl.BlockSpec(memory_space=pl.ANY)
    held = pl.BlockSpec(memory_space=pltpu.VMEM)
    dma = pltpu.SemaphoreType.DMA
    ready = pl.pallas_call(
        prepare,
        out_shape=(
            pltpu.VMEM((512, 256), F32),
            pltpu.VMEM((2, 2, 128, 256), F32),
            pltpu.VMEM((8, 128), F32),
            pltpu.VMEM(base.shape, BF16),
            pltpu.VMEM(last.shape[1:], BF16),
            pltpu.VMEM(twist.shape, F32),
        ),
        in_specs=[anywhere] * 11,
        out_specs=(held,) * 6,
        scratch_shapes=[
            pltpu.SMEM((2,), jnp.int32),
            pltpu.SMEM((2,), F32),
            pltpu.SMEM((2,), F32),
            pltpu.SMEM((48,), jnp.int32),
            pltpu.VMEM((384, 128), F32),
            pltpu.VMEM((256, 128), F32),
            pltpu.VMEM((2, 512, 128), BF16),
            pltpu.VMEM(pick.shape, BF16),
            pltpu.VMEM((384, 128), F32),
            pltpu.VMEM((128, 128), F32),
            dma((12,)),
            dma((2,)),
        ],
        compiler_params=pltpu.CompilerParams(
            collective_id=0, has_side_effects=True, vmem_limit_bytes=56 * 1024 * 1024
        ),
    )(
        tmpl_len, weights, chirp_mass, valid,
        strain.reshape(384, 128), inv_asd.reshape(256, 128), dealt, base, last, twist, pick,
    )
    mine_log, mine_chirp, mine_delay, other_log, other_chirp, other_delay, log_prior = pl.pallas_call(
        match,
        out_shape=(pltpu.VMEM((24, 128), F32),) * 7,
        in_specs=[held] * 6,
        out_specs=(held,) * 7,
        scratch_shapes=[
            pltpu.VMEM((HALVES, GROUP, 24, 256), F32),
            pltpu.VMEM((HALVES, GROUP, 24, 256), F32),
            pltpu.VMEM((GROUP, 8, 128), F32),
            pltpu.VMEM((80, 128), F32),
            pltpu.VMEM((80, 128), F32),
            dma((HALVES, GROUP)),
            dma((HALVES, GROUP)),
            dma((GROUP,)),
            dma((GROUP,)),
            dma((2,)),
        ],
        compiler_params=pltpu.CompilerParams(
            collective_id=1, has_side_effects=True, vmem_limit_bytes=56 * 1024 * 1024
        ),
    )(*[pltpu.with_memory_space_constraint(array, pltpu.VMEM) for array in ready])
    peak = jnp.maximum(mine_log, other_log)
    mass_a, mass_b = jnp.exp(mine_log - peak), jnp.exp(other_log - peak)
    total = mass_a + mass_b
    outs = (
        peak + jnp.log(total) - log_prior,
        (mass_a * mine_chirp + mass_b * other_chirp) / total,
        (mass_a * mine_delay + mass_b * other_delay) / total,
    )
    return tuple(out.reshape(3072) for out in outs)


def solution(mesh):
    placed = (P("seg"), P(), P(None, "bank", None), P("bank"), P("bank"), P("bank"), P("seg"))
    return jax.shard_map(
        local,
        mesh=mesh,
        in_specs=placed,
        out_specs=(P(("seg", "bank")), P(("seg", "bank")), P(("seg", "bank"))),
        check_vma=False,
    )
```

```python
import functools
import math

import jax
import jax.numpy as jnp
import ml_dtypes
import numpy as np
from jax import lax
from jax.experimental import pallas as pl
from jax.experimental.pallas import tpu as pltpu
from jax.sharding import PartitionSpec as P

NFFT = 65536
OVER = 16384
RATE = 4096
HOP = 49152
F32, BF16 = jnp.float32, jnp.bfloat16
MESH = pl.DeviceIdType.MESH
HALVES = 2
GROUP = 8


def halves(table):
    high = table.astype(ml_dtypes.bfloat16)
    low = (table - high.astype(np.float64)).astype(ml_dtypes.bfloat16)
    return high, low


@functools.cache
def tables():
    turn = np.outer(np.arange(256), np.arange(256)) % 256 * (2 * np.pi / 256)
    base = np.stack(halves(np.concatenate([np.cos(turn), np.sin(turn)])))
    last = []
    for z in range(2):
        order = []
        for half in (1 - z, z):
            begins = [48 * y + 24 * half + 12 * core for y in range(4) for core in range(2)]
            order += [t + i for t in begins for i in range(8)] + [t + i for t in begins for i in range(8, 12)]
        last.append(halves(np.concatenate([np.cos(turn)[order], np.sin(turn)[order]])))
    last = np.array(last)
    twist = np.outer(np.arange(256), np.arange(256)) * (2 * np.pi / NFFT)
    twist = np.stack([np.cos(twist), np.sin(twist)]).astype(np.float32)
    pick = np.zeros((128, 128), ml_dtypes.bfloat16)
    for k in range(2):
        for h in range(2):
            for a in range(32):
                pick[k * 64 + h * 32 + a, (2 * a + h) * 2 + k] = 1
    return base, last, twist, pick


def split(value):
    high = value.astype(BF16)
    return high, (value - high.astype(F32)).astype(BF16)


def mul(left, right):
    return lax.dot_general(left, right, (((1,), (0,)), ((), ())), preferred_element_type=F32)


def mul_t(left, right):
    return lax.dot_general(left, right, (((1,), (1,)), ((), ())), preferred_element_type=F32)


def cos_sin_turn(fraction):
    half = (fraction - jnp.where(fraction >= 0.5, 1.0, 0.0)) * math.pi
    sq = half * half
    s = 1.0 / 6227020800.0
    for term in (-1.0 / 39916800.0, 1.0 / 362880.0, -1.0 / 5040.0, 1.0 / 120.0, -1.0 / 6.0, 1.0):
        s = s * sq + term
    s = s * half
    c = -1.0 / 87178291200.0
    for term in (
        1.0 / 479001600.0,
        -1.0 / 3628800.0,
        1.0 / 40320.0,
        -1.0 / 720.0,
        1.0 / 24.0,
        -0.5,
        1.0,
    ):
        c = c * sq + term
    return 1.0 - 2.0 * s * s, 2.0 * s * c


def log_bessel(power):
    edge = 3.75 * 3.75
    t = jnp.minimum(power, edge) * (1.0 / edge)
    small = jnp.full_like(t, 0.0045813)
    for term in (0.0360768, 0.2659732, 1.2067492, 3.0899424, 3.5156229, 1.0):
        small = small * t + term
    above = jnp.maximum(power, edge)
    inverse = lax.rsqrt(above)
    x = above * inverse
    q = 3.75 * inverse
    large = jnp.full_like(t, 0.00392377)
    for term in (
        -0.01647633,
        0.02635537,
        -0.02057706,
        0.00916281,
        -0.00157565,
        0.00225319,
        0.01328592,
        0.39894228,
    ):
        large = large * q + term
    is_small = power < edge
    return jnp.where(is_small, 0.0, x) + jnp.log(
        jnp.where(is_small, small, large * lax.rsqrt(x))
    )


def frame(ref, begin, count):
    return jnp.concatenate([ref[pl.ds(begin, count, 2), :], ref[pl.ds(begin + 1, count, 2), :]], axis=1)


def turning(cos, sin):
    return jnp.concatenate(
        [jnp.concatenate([cos, -sin], axis=1), jnp.concatenate([sin, cos], axis=1)], axis=0
    )


def thrice(high, low):
    return jnp.concatenate([high, low, high], axis=1)


def prepare(
    len_hbm, weight_hbm, mass_hbm, valid_hbm, strain_hbm, asd_hbm, tmpl_hbm, base_hbm, last_hbm, twist_hbm, pick_hbm,
    part_out, filt, trait, base, last, twist,
    len_ref, weight_ref, mass_ref, valid_ref, strain, asd, tmpl, pick, gated, halo, in_sem, halo_sem,
):
    seg, bank = lax.axis_index("seg"), lax.axis_index("bank")
    seg_count = lax.axis_size("seg")
    barrier = pltpu.get_barrier_semaphore()

    @pl.when(seg > 0)
    def _():
        pl.semaphore_signal(barrier, inc=1, device_id=(seg - 1, bank), device_id_type=MESH)

    pairs = (
        (valid_hbm, valid_ref),
        (strain_hbm.at[256:384], strain.at[256:384]),
        (strain_hbm.at[0:256], strain.at[0:256]),
        (base_hbm, base),
        (len_hbm, len_ref),
        (weight_hbm, weight_ref),
        (mass_hbm, mass_ref),
        (pick_hbm, pick),
        (tmpl_hbm, tmpl),
        (asd_hbm, asd),
        (twist_hbm, twist),
        (last_hbm.at[bank // 2 % 2], last),
    )
    loads = [pltpu.make_async_copy(source, target, in_sem.at[i]) for i, (source, target) in enumerate(pairs)]
    loads[0].start()
    loads[1].start()
    for load in loads[2:]:
        load.start()

    def gate(begin, end):
        for i in range(begin, end):
            gated[8 * i : 8 * i + 8, :] = strain[8 * i : 8 * i + 8, :] * valid_ref[i].astype(F32)

    loads[0].wait()
    loads[1].wait()
    gate(32, 48)

    def halo_copy():
        return pltpu.make_async_remote_copy(
            src_ref=gated.at[256:384], dst_ref=halo, send_sem=halo_sem.at[0], recv_sem=halo_sem.at[1],
            device_id=(seg + 1, bank), device_id_type=MESH,
        )

    @pl.when(seg < seg_count - 1)
    def _():
        pl.semaphore_wait(barrier, 1)
        halo_copy().start()

    @pl.when(seg == 0)
    def _():
        halo[...] = jnp.zeros((128, 128), F32)

    for i in range(4, 7):
        loads[i].wait()
    lane = lax.broadcasted_iota(jnp.int32, (1, 128), 1)
    facts = (
        weight_ref[0] + weight_ref[1],
        mass_ref[0],
        mass_ref[1],
        len_ref[0].astype(F32) * (1.0 / RATE),
        len_ref[1].astype(F32) * (1.0 / RATE),
        weight_ref[0],
        weight_ref[1],
    )
    tile = jnp.zeros((1, 128), F32)
    for i, fact in enumerate(facts):
        tile = jnp.where(lane == i, fact, tile)
    trait[...] = tile

    loads[2].wait()
    gate(0, 32)
    high, low = split(frame(gated, 0, 192))
    loads[3].wait()
    blank = jnp.zeros((64, 256), BF16)
    first = thrice(base[0], base[1])
    part = mul(first, jnp.concatenate([blank, high, blank, high, blank, low], axis=0))

    loads[7].wait()
    loads[8].wait()
    deal = []
    for i in range(4):
        rows = slice(128 * i, 128 * i + 128)
        deal.append(mul(pick[...], jnp.concatenate([tmpl[0, rows], tmpl[1, rows]], axis=1)))
    loads[9].wait()
    level = frame(asd, 0, 128)
    for k in range(2):
        parts = [
            jnp.concatenate([d[64 * k + 32 * h : 64 * k + 32 * h + 32] for d in deal], axis=0) for h in range(2)
        ]
        tmpl_re = jnp.concatenate([p[:, :128] for p in parts], axis=1)
        tmpl_im = jnp.concatenate([p[:, 128:] for p in parts], axis=1)
        sigma = jnp.sum(level * level * (tmpl_re * tmpl_re + tmpl_im * tmpl_im), keepdims=True)
        start = OVER - len_ref[k]
        index = lax.broadcasted_iota(jnp.int32, (128, 128), 0) * start % 256
        long_cos, long_sin = cos_sin_turn(index.astype(F32) * (1.0 / 256))
        index = lax.broadcasted_iota(jnp.int32, (1, 256), 1) * start % NFFT
        short_cos, short_sin = cos_sin_turn(index.astype(F32) * (1.0 / NFFT))
        long_cos = jnp.concatenate([long_cos, long_cos], axis=1)
        long_sin = jnp.concatenate([long_sin, long_sin], axis=1)
        turn_re = long_cos * short_cos - long_sin * short_sin
        turn_im = long_cos * short_sin + long_sin * short_cos
        scale = level * (lax.rsqrt(sigma) * (1.0 / math.sqrt(NFFT)))
        filt[k, 0] = (tmpl_re * turn_re + tmpl_im * turn_im) * scale
        filt[k, 1] = (tmpl_re * turn_im - tmpl_im * turn_re) * scale
    loads[10].wait()
    loads[11].wait()

    @pl.when(seg > 0)
    def _():
        halo_copy().wait_recv()

    high, low = split(frame(halo, 0, 64))
    part_out[...] = part + mul(
        thrice(base[0, :, 0:128], base[1, :, 0:128]),
        jnp.concatenate([high, blank, high, blank, low, blank], axis=0),
    )

    @pl.when(seg < seg_count - 1)
    def _():
        halo_copy().wait_send()


def match(
    part, filt, trait, base, last, twist,
    mine_log, mine_chirp, mine_delay, other_log, other_chirp, other_delay, log_prior,
    send, recv, traits, packet, arrived, send_sem, recv_sem, trait_send, trait_recv, z_sem,
):
    seg, bank = lax.axis_index("seg"), lax.axis_index("bank")
    y, z, core = bank // 4, bank // 2 % 2, bank % 2
    rank = y * 2 + core

    def bank_of(rank_, z_):
        return rank_ // 2 * 4 + z_ * 2 + rank_ % 2

    barrier = pltpu.get_barrier_semaphore()
    peers = [(seg, bank_of((rank + o) % GROUP, z)) for o in range(1, GROUP)]
    opposite = (seg, bank_of(rank, 1 - z))
    for peer in [peers[o - 1] for o in (4, 5, 3, 2, 6, 7, 1)] + [opposite]:
        pl.semaphore_signal(barrier, inc=1, device_id=peer, device_id_type=MESH)
    twist_cos, twist_sin = twist[0], twist[1]

    turned = jnp.concatenate(
        [
            part[0:256] * twist_cos - part[256:512] * twist_sin,
            part[256:512] * twist_cos + part[0:256] * twist_sin,
        ],
        axis=1,
    )
    high, low = split(turned)
    second = [turning(base[i, 0:128], base[i, 256:384]) for i in range(2)]
    spec = mul_t(jnp.concatenate(second, axis=0), high)
    spec = spec[:256] + spec[256:] + mul_t(second[0], low)
    spec_re, spec_im = spec[:128], spec[128:]
    third = thrice(*[turning(base[i, 0:256, 0:128], base[i, 256:512, 0:128]) for i in range(2)])
    weights = []
    for k in range(2):
        filt_re, filt_im = filt[k, 0], filt[k, 1]
        prod = jnp.concatenate(
            [spec_re * filt_re + spec_im * filt_im, spec_re * filt_im - spec_im * filt_re], axis=0
        )
        high, low = split(prod)
        inner = mul(third, jnp.concatenate([high, high, low], axis=0))
        turned = jnp.concatenate(
            [
                inner[:256] * twist_cos - inner[256:] * twist_sin,
                inner[:256] * twist_sin + inner[256:] * twist_cos,
            ],
            axis=1,
        )
        high, low = split(turned)
        weights.append((high, low))

    def score_copy(piece, o):
        rows = ((0, slice(0, 16)), (0, slice(16, 24)), (1, slice(0, 24)))[piece]
        j, part_of = rows
        return pltpu.make_async_remote_copy(
            src_ref=send.at[j, (rank + o) % GROUP, part_of], dst_ref=recv.at[j, o, part_of],
            send_sem=send_sem.at[piece, o], recv_sem=recv_sem.at[piece, o],
            device_id=peers[o - 1], device_id_type=MESH,
        )

    trait_copies = [
        pltpu.make_async_remote_copy(
            src_ref=trait, dst_ref=traits.at[o], send_sem=trait_send.at[o], recv_sem=trait_recv.at[o],
            device_id=peers[o - 1], device_id_type=MESH,
        )
        for o in range(1, GROUP)
    ]
    log_weight = [jnp.log(jnp.broadcast_to(trait[0:1, 5 + k : 6 + k], (8, 256))) for k in range(2)]
    for j in range(HALVES):
        fourth = [turning(last[i, 96 * j : 96 * j + 96], last[i, 96 * j + 192 : 96 * j + 288]) for i in range(2)]
        stacked = jnp.concatenate(fourth, axis=0)
        for k in range(2):
            high, low = weights[k]
            corr = mul_t(stacked, high)
            corr = corr[:192] + corr[192:] + mul_t(fourth[0], low)

            def score(p):
                re, im = corr[p : p + 8], corr[p + 96 : p + 104]
                return log_bessel(re * re + im * im) + log_weight[k]

            for block in range(GROUP):
                send[j, block, 8 * k : 8 * k + 8] = score(8 * block)
            for block in range(0, GROUP, 2):
                both = score(64 + 4 * block)
                send[j, block, 16 + 4 * k : 20 + 4 * k] = both[:4]
                send[j, block + 1, 16 + 4 * k : 20 + 4 * k] = both[4:]
        if j == 0:
            pl.semaphore_wait(barrier, GROUP)
            for o in (4, 5, 3, 2, 6, 7, 1):
                score_copy(0, o).start()
            for copy in trait_copies:
                copy.start()
            for o in (4, 5, 3, 2, 6, 7, 1):
                score_copy(1, o).start()

    def z_copy(i):
        rows = (slice(0, 48), slice(48, 80))[i]
        return pltpu.make_async_remote_copy(
            src_ref=packet.at[rows], dst_ref=arrived.at[rows], send_sem=z_sem.at[i], recv_sem=z_sem.at[2 + i],
            device_id=opposite, device_id_type=MESH,
        )

    def arrivals(j, begin):
        return [send[j, rank, begin : begin + 8]] + [recv[j, o, begin : begin + 8] for o in range(1, GROUP)]

    def fact(o, i):
        return traits[o, 0:1, i : i + 1]

    def upper(j):
        scores = [arrivals(j, 0), arrivals(j, 8)]
        peak = functools.reduce(jnp.maximum, scores[0] + scores[1])
        total = chirp_sum = delay_sum = jnp.zeros((8, 256), F32)
        for o in range(GROUP):
            for k in range(2):
                mass = jnp.exp(scores[k][o] - peak)
                total = total + mass
                chirp_sum = chirp_sum + mass * fact(o, 1 + k)
                delay_sum = delay_sum + mass * fact(o, 3 + k)
        inverse = 1.0 / total
        return peak + jnp.log(total), chirp_sum * inverse, delay_sum * inverse

    is_first = lax.broadcasted_iota(jnp.int32, (8, 256), 0) < 4

    def lower(j):
        scores = arrivals(j, 16)
        peak = functools.reduce(jnp.maximum, scores)
        peak = jnp.maximum(peak[:4], peak[4:])
        peak_twice = jnp.concatenate([peak, peak], axis=0)
        total = chirp_sum = delay_sum = jnp.zeros((8, 256), F32)
        for o in range(GROUP):
            mass = jnp.exp(scores[o] - peak_twice)
            total = total + mass
            chirp_sum = chirp_sum + mass * jnp.where(is_first, fact(o, 1), fact(o, 2))
            delay_sum = delay_sum + mass * jnp.where(is_first, fact(o, 3), fact(o, 4))
        total, chirp_sum, delay_sum = [v[:4] + v[4:] for v in (total, chirp_sum, delay_sum)]
        inverse = 1.0 / total
        return peak + jnp.log(total), chirp_sum * inverse, delay_sum * inverse

    def landed(piece):
        for o in range(1, GROUP):
            score_copy(piece, o).wait_recv()

    for copy in trait_copies:
        copy.wait_recv()
    traits[0] = trait[...]
    landed(0)
    for i, value in enumerate(upper(0)):
        for h in range(2):
            packet[pl.ds(16 * i + h, 8, 2), :] = value[:, 128 * h : 128 * h + 128]
    z_copy(0).start()
    weight_sum = fact(0, 0)
    for o in range(1, GROUP):
        weight_sum = weight_sum + fact(o, 0)
    packet[72:80] = jnp.broadcast_to(weight_sum, (8, 128))
    landed(1)
    for o in (4, 5, 3, 2, 6, 7, 1):
        score_copy(2, o).start()
    for i, value in enumerate(lower(0)):
        for h in range(2):
            packet[pl.ds(48 + 8 * i + h, 4, 2), :] = value[:, 128 * h : 128 * h + 128]
    z_copy(1).start()
    landed(2)
    for out, high, low in zip((mine_log, mine_chirp, mine_delay), upper(1), lower(1)):
        for h in range(2):
            lanes = slice(128 * h, 128 * h + 128)
            out[pl.ds(h, 8, 2), :] = high[:, lanes]
            out[pl.ds(16 + h, 4, 2), :] = low[:, lanes]

    for copy in trait_copies:
        copy.wait_send()
    for piece in range(3):
        for o in range(1, GROUP):
            score_copy(piece, o).wait_send()
    for i in range(2):
        z_copy(i).wait()
    for i, out in enumerate((other_log, other_chirp, other_delay)):
        out[0:16] = arrived[16 * i : 16 * i + 16]
        out[16:24] = arrived[48 + 8 * i : 56 + 8 * i]
    level = jnp.log(packet[72:80] + arrived[72:80])
    for i in range(3):
        log_prior[8 * i : 8 * i + 8] = level


def local(strain, inv_asd, templates, tmpl_len, weights, chirp_mass, valid):
    base, last, twist, pick = tables()
    dealt = templates.reshape(2, 2, 256, 128).transpose(0, 2, 1, 3).reshape(2, 512, 128)
    anywhere = pl.BlockSpec(memory_space=pl.ANY)
    held = pl.BlockSpec(memory_space=pltpu.VMEM)
    dma = pltpu.SemaphoreType.DMA
    ready = pl.pallas_call(
        prepare,
        out_shape=(
            pltpu.VMEM((512, 256), F32),
            pltpu.VMEM((2, 2, 128, 256), F32),
            pltpu.VMEM((1, 128), F32),
            pltpu.VMEM(base.shape, BF16),
            pltpu.VMEM(last.shape[1:], BF16),
            pltpu.VMEM(twist.shape, F32),
        ),
        in_specs=[anywhere] * 11,
        out_specs=(held,) * 6,
        scratch_shapes=[
            pltpu.SMEM((2,), jnp.int32),
            pltpu.SMEM((2,), F32),
            pltpu.SMEM((2,), F32),
            pltpu.SMEM((48,), jnp.int32),
            pltpu.VMEM((384, 128), F32),
            pltpu.VMEM((256, 128), F32),
            pltpu.VMEM((2, 512, 128), BF16),
            pltpu.VMEM(pick.shape, BF16),
            pltpu.VMEM((384, 128), F32),
            pltpu.VMEM((128, 128), F32),
            dma((12,)),
            dma((2,)),
        ],
        compiler_params=pltpu.CompilerParams(
            collective_id=0, has_side_effects=True, vmem_limit_bytes=56 * 1024 * 1024
        ),
    )(
        tmpl_len, weights, chirp_mass, valid,
        strain.reshape(384, 128), inv_asd.reshape(256, 128), dealt, base, last, twist, pick,
    )
    mine_log, mine_chirp, mine_delay, other_log, other_chirp, other_delay, log_prior = pl.pallas_call(
        match,
        out_shape=(pltpu.VMEM((24, 128), F32),) * 7,
        in_specs=[held] * 6,
        out_specs=(held,) * 7,
        scratch_shapes=[
            pltpu.VMEM((HALVES, GROUP, 24, 256), F32),
            pltpu.VMEM((HALVES, GROUP, 24, 256), F32),
            pltpu.VMEM((GROUP, 1, 128), F32),
            pltpu.VMEM((80, 128), F32),
            pltpu.VMEM((80, 128), F32),
            dma((3, GROUP)),
            dma((3, GROUP)),
            dma((GROUP,)),
            dma((GROUP,)),
            dma((4,)),
        ],
        compiler_params=pltpu.CompilerParams(
            collective_id=1, has_side_effects=True, vmem_limit_bytes=56 * 1024 * 1024
        ),
    )(*[pltpu.with_memory_space_constraint(array, pltpu.VMEM) for array in ready])
    peak = jnp.maximum(mine_log, other_log)
    mass_a, mass_b = jnp.exp(mine_log - peak), jnp.exp(other_log - peak)
    total = mass_a + mass_b
    outs = (
        peak + jnp.log(total) - log_prior,
        (mass_a * mine_chirp + mass_b * other_chirp) / total,
        (mass_a * mine_delay + mass_b * other_delay) / total,
    )
    return tuple(out.reshape(3072) for out in outs)


def solution(mesh):
    placed = (P("seg"), P(), P(None, "bank", None), P("bank"), P("bank"), P("bank"), P("seg"))
    return jax.shard_map(
        local,
        mesh=mesh,
        in_specs=placed,
        out_specs=(P(("seg", "bank")), P(("seg", "bank")), P(("seg", "bank"))),
        check_vma=False,
    )
```

```python
import functools
import math

import jax
import jax.numpy as jnp
import ml_dtypes
import numpy as np
from jax import lax
from jax.experimental import pallas as pl
from jax.experimental.pallas import tpu as pltpu
from jax.sharding import PartitionSpec as P

NFFT = 65536
OVER = 16384
RATE = 4096
HOP = 49152
F32, BF16 = jnp.float32, jnp.bfloat16
MESH = pl.DeviceIdType.MESH
HALVES = 2
GROUP = 8


def halves(table):
    high = table.astype(ml_dtypes.bfloat16)
    low = (table - high.astype(np.float64)).astype(ml_dtypes.bfloat16)
    return high, low


@functools.cache
def tables():
    turn = np.outer(np.arange(256), np.arange(256)) % 256 * (2 * np.pi / 256)
    base = np.stack(halves(np.concatenate([np.cos(turn), np.sin(turn)])))
    last = []
    for z in range(2):
        order = []
        for half in (1 - z, z):
            begins = [48 * y + 24 * half + 12 * core for y in range(4) for core in range(2)]
            order += [t + i for t in begins for i in range(8)] + [t + i for t in begins for i in range(8, 12)]
        last.append(halves(np.concatenate([np.cos(turn)[order], np.sin(turn)[order]])))
    last = np.array(last)
    twist = np.outer(np.arange(256), np.arange(256)) * (2 * np.pi / NFFT)
    twist = np.stack([np.cos(twist), np.sin(twist)]).astype(np.float32)
    pick = np.zeros((128, 128), ml_dtypes.bfloat16)
    for k in range(2):
        for h in range(2):
            for a in range(32):
                pick[k * 64 + h * 32 + a, (2 * a + h) * 2 + k] = 1
    return base, last, twist, pick


def split(value):
    high = value.astype(BF16)
    return high, (value - high.astype(F32)).astype(BF16)


def mul(left, right):
    return lax.dot_general(left, right, (((1,), (0,)), ((), ())), preferred_element_type=F32)


def mul_t(left, right):
    return lax.dot_general(left, right, (((1,), (1,)), ((), ())), preferred_element_type=F32)


def cos_sin_turn(fraction):
    half = (fraction - jnp.where(fraction >= 0.5, 1.0, 0.0)) * math.pi
    sq = half * half
    s = 1.0 / 6227020800.0
    for term in (-1.0 / 39916800.0, 1.0 / 362880.0, -1.0 / 5040.0, 1.0 / 120.0, -1.0 / 6.0, 1.0):
        s = s * sq + term
    s = s * half
    c = -1.0 / 87178291200.0
    for term in (
        1.0 / 479001600.0,
        -1.0 / 3628800.0,
        1.0 / 40320.0,
        -1.0 / 720.0,
        1.0 / 24.0,
        -0.5,
        1.0,
    ):
        c = c * sq + term
    return 1.0 - 2.0 * s * s, 2.0 * s * c


def log_bessel(power):
    edge = 3.75 * 3.75
    t = jnp.minimum(power, edge) * (1.0 / edge)
    small = jnp.full_like(t, 0.0045813)
    for term in (0.0360768, 0.2659732, 1.2067492, 3.0899424, 3.5156229, 1.0):
        small = small * t + term
    above = jnp.maximum(power, edge)
    inverse = lax.rsqrt(above)
    x = above * inverse
    q = 3.75 * inverse
    large = jnp.full_like(t, 0.00392377)
    for term in (
        -0.01647633,
        0.02635537,
        -0.02057706,
        0.00916281,
        -0.00157565,
        0.00225319,
        0.01328592,
        0.39894228,
    ):
        large = large * q + term
    is_small = power < edge
    return jnp.where(is_small, 0.0, x) + jnp.log(
        jnp.where(is_small, small, large * lax.rsqrt(x))
    )


def frame(ref, begin, count):
    return jnp.concatenate([ref[pl.ds(begin, count, 2), :], ref[pl.ds(begin + 1, count, 2), :]], axis=1)


def turning(cos, sin):
    return jnp.concatenate(
        [jnp.concatenate([cos, -sin], axis=1), jnp.concatenate([sin, cos], axis=1)], axis=0
    )


def thrice(high, low):
    return jnp.concatenate([high, low, high], axis=1)


def prepare(
    len_hbm, weight_hbm, mass_hbm, valid_hbm, strain_hbm, asd_hbm, tmpl_hbm, base_hbm, last_hbm, twist_hbm, pick_hbm,
    part_out, filt, trait, base, last, twist,
    len_ref, weight_ref, mass_ref, valid_ref, strain, asd, tmpl, pick, gated, halo, in_sem, halo_sem,
):
    seg, bank = lax.axis_index("seg"), lax.axis_index("bank")
    seg_count = lax.axis_size("seg")
    barrier = pltpu.get_barrier_semaphore()

    @pl.when(seg > 0)
    def _():
        pl.semaphore_signal(barrier, inc=1, device_id=(seg - 1, bank), device_id_type=MESH)

    pairs = (
        (valid_hbm, valid_ref),
        (strain_hbm.at[256:384], strain.at[256:384]),
        (strain_hbm.at[0:256], strain.at[0:256]),
        (base_hbm, base),
        (len_hbm, len_ref),
        (weight_hbm, weight_ref),
        (mass_hbm, mass_ref),
        (pick_hbm, pick),
        (tmpl_hbm, tmpl),
        (asd_hbm, asd),
        (twist_hbm, twist),
        (last_hbm.at[bank // 2 % 2], last),
    )
    loads = [pltpu.make_async_copy(source, target, in_sem.at[i]) for i, (source, target) in enumerate(pairs)]
    loads[0].start()
    loads[1].start()
    for load in loads[2:]:
        load.start()

    def gate(begin, end):
        for i in range(begin, end):
            gated[8 * i : 8 * i + 8, :] = strain[8 * i : 8 * i + 8, :] * valid_ref[i].astype(F32)

    loads[0].wait()
    loads[1].wait()
    gate(32, 48)

    def halo_copy():
        return pltpu.make_async_remote_copy(
            src_ref=gated.at[256:384], dst_ref=halo, send_sem=halo_sem.at[0], recv_sem=halo_sem.at[1],
            device_id=(seg + 1, bank), device_id_type=MESH,
        )

    @pl.when(seg < seg_count - 1)
    def _():
        pl.semaphore_wait(barrier, 1)
        halo_copy().start()

    @pl.when(seg == 0)
    def _():
        halo[...] = jnp.zeros((128, 128), F32)

    for i in range(4, 7):
        loads[i].wait()
    lane = lax.broadcasted_iota(jnp.int32, (1, 128), 1)
    facts = (
        weight_ref[0] + weight_ref[1],
        mass_ref[0],
        mass_ref[1],
        len_ref[0].astype(F32) * (1.0 / RATE),
        len_ref[1].astype(F32) * (1.0 / RATE),
        weight_ref[0],
        weight_ref[1],
    )
    tile = jnp.zeros((1, 128), F32)
    for i, fact in enumerate(facts):
        tile = jnp.where(lane == i, fact, tile)
    trait[...] = tile

    loads[2].wait()
    gate(0, 32)
    high, low = split(frame(gated, 0, 192))
    loads[3].wait()
    blank = jnp.zeros((64, 256), BF16)
    first = thrice(base[0], base[1])
    part = mul(first, jnp.concatenate([blank, high, blank, high, blank, low], axis=0))

    loads[7].wait()
    loads[8].wait()
    deal = []
    for i in range(4):
        rows = slice(128 * i, 128 * i + 128)
        deal.append(mul(pick[...], jnp.concatenate([tmpl[0, rows], tmpl[1, rows]], axis=1)))
    loads[9].wait()
    level = frame(asd, 0, 128)
    for k in range(2):
        parts = [
            jnp.concatenate([d[64 * k + 32 * h : 64 * k + 32 * h + 32] for d in deal], axis=0) for h in range(2)
        ]
        tmpl_re = jnp.concatenate([p[:, :128] for p in parts], axis=1)
        tmpl_im = jnp.concatenate([p[:, 128:] for p in parts], axis=1)
        sigma = jnp.sum(level * level * (tmpl_re * tmpl_re + tmpl_im * tmpl_im), keepdims=True)
        start = OVER - len_ref[k]
        index = lax.broadcasted_iota(jnp.int32, (128, 128), 0) * start % 256
        long_cos, long_sin = cos_sin_turn(index.astype(F32) * (1.0 / 256))
        index = lax.broadcasted_iota(jnp.int32, (1, 256), 1) * start % NFFT
        short_cos, short_sin = cos_sin_turn(index.astype(F32) * (1.0 / NFFT))
        long_cos = jnp.concatenate([long_cos, long_cos], axis=1)
        long_sin = jnp.concatenate([long_sin, long_sin], axis=1)
        turn_re = long_cos * short_cos - long_sin * short_sin
        turn_im = long_cos * short_sin + long_sin * short_cos
        scale = level * (lax.rsqrt(sigma) * (1.0 / math.sqrt(NFFT)))
        filt[k, 0] = (tmpl_re * turn_re + tmpl_im * turn_im) * scale
        filt[k, 1] = (tmpl_re * turn_im - tmpl_im * turn_re) * scale
    loads[10].wait()
    loads[11].wait()

    @pl.when(seg > 0)
    def _():
        halo_copy().wait_recv()

    high, low = split(frame(halo, 0, 64))
    part_out[...] = part + mul(
        thrice(base[0, :, 0:128], base[1, :, 0:128]),
        jnp.concatenate([high, blank, high, blank, low, blank], axis=0),
    )

    @pl.when(seg < seg_count - 1)
    def _():
        halo_copy().wait_send()


def match(
    part, filt, trait, base, last, twist,
    mine_log, mine_chirp, mine_delay, other_log, other_chirp, other_delay, log_prior,
    send, recv, traits, packet, arrived, send_sem, recv_sem, trait_send, trait_recv, z_sem,
):
    seg, bank = lax.axis_index("seg"), lax.axis_index("bank")
    y, z, core = bank // 4, bank // 2 % 2, bank % 2
    rank = y * 2 + core

    def bank_of(rank_, z_):
        return rank_ // 2 * 4 + z_ * 2 + rank_ % 2

    barrier = pltpu.get_barrier_semaphore()
    peers = [(seg, bank_of((rank + o) % GROUP, z)) for o in range(1, GROUP)]
    opposite = (seg, bank_of(rank, 1 - z))
    for peer in [opposite] + peers:
        pl.semaphore_signal(barrier, inc=1, device_id=peer, device_id_type=MESH)
    twist_cos, twist_sin = twist[0], twist[1]

    turned = jnp.concatenate(
        [
            part[0:256] * twist_cos - part[256:512] * twist_sin,
            part[256:512] * twist_cos + part[0:256] * twist_sin,
        ],
        axis=1,
    )
    high, low = split(turned)
    second = [turning(base[i, 0:128], base[i, 256:384]) for i in range(2)]
    spec = mul_t(jnp.concatenate(second, axis=0), high)
    spec = spec[:256] + spec[256:] + mul_t(second[0], low)
    spec_re, spec_im = spec[:128], spec[128:]
    third = thrice(*[turning(base[i, 0:256, 0:128], base[i, 256:512, 0:128]) for i in range(2)])
    weights = []
    for k in range(2):
        filt_re, filt_im = filt[k, 0], filt[k, 1]
        prod = jnp.concatenate(
            [spec_re * filt_re + spec_im * filt_im, spec_re * filt_im - spec_im * filt_re], axis=0
        )
        high, low = split(prod)
        inner = mul(third, jnp.concatenate([high, high, low], axis=0))
        turned = jnp.concatenate(
            [
                inner[:256] * twist_cos - inner[256:] * twist_sin,
                inner[:256] * twist_sin + inner[256:] * twist_cos,
            ],
            axis=1,
        )
        high, low = split(turned)
        weights.append((high, low))

    def score_copy(j, o):
        return pltpu.make_async_remote_copy(
            src_ref=send.at[j, (rank + o) % GROUP], dst_ref=recv.at[j, o],
            send_sem=send_sem.at[j, o], recv_sem=recv_sem.at[j, o],
            device_id=peers[o - 1], device_id_type=MESH,
        )

    trait_copies = [
        pltpu.make_async_remote_copy(
            src_ref=trait, dst_ref=traits.at[o], send_sem=trait_send.at[o], recv_sem=trait_recv.at[o],
            device_id=peers[o - 1], device_id_type=MESH,
        )
        for o in range(1, GROUP)
    ]
    log_weight = [jnp.log(jnp.broadcast_to(trait[0:1, 5 + k : 6 + k], (8, 256))) for k in range(2)]
    for j in range(HALVES):
        fourth = [turning(last[i, 96 * j : 96 * j + 96], last[i, 96 * j + 192 : 96 * j + 288]) for i in range(2)]
        stacked = jnp.concatenate(fourth, axis=0)
        for k in range(2):
            high, low = weights[k]
            corr = mul_t(stacked, high)
            corr = corr[:192] + corr[192:] + mul_t(fourth[0], low)

            def score(p):
                re, im = corr[p : p + 8], corr[p + 96 : p + 104]
                return log_bessel(re * re + im * im) + log_weight[k]

            for block in range(GROUP):
                send[j, block, 8 * k : 8 * k + 8] = score(8 * block)
            for block in range(0, GROUP, 2):
                both = score(64 + 4 * block)
                send[j, block, 16 + 4 * k : 20 + 4 * k] = both[:4]
                send[j, block + 1, 16 + 4 * k : 20 + 4 * k] = both[4:]
        if j == 0:
            pl.semaphore_wait(barrier, GROUP)
            for o in (4, 5, 3, 2, 6, 7, 1):
                score_copy(0, o).start()
            for copy in trait_copies:
                copy.start()

    for copy in trait_copies:
        copy.wait_recv()
    traits[0] = trait[...]
    weight_sum = traits[0, 0:1, 0:1]
    for o in range(1, GROUP):
        weight_sum = weight_sum + traits[o, 0:1, 0:1]
    packet[72:80] = jnp.broadcast_to(weight_sum, (8, 128))

    z_copy = pltpu.make_async_remote_copy(
        src_ref=packet, dst_ref=arrived, send_sem=z_sem.at[0], recv_sem=z_sem.at[1],
        device_id=opposite, device_id_type=MESH,
    )
    is_first = lax.broadcasted_iota(jnp.int32, (8, 256), 0) < 4
    for j in range(HALVES):
        for o in range(1, GROUP):
            score_copy(j, o).wait_recv()
        if j == 0:
            for o in (4, 5, 3, 2, 6, 7, 1):
                score_copy(1, o).start()

        def arrivals(begin):
            return [send[j, rank, begin : begin + 8]] + [recv[j, o, begin : begin + 8] for o in range(1, GROUP)]

        def fact(o, i):
            return traits[o, 0:1, i : i + 1]

        scores = [arrivals(0), arrivals(8)]
        peak = functools.reduce(jnp.maximum, scores[0] + scores[1])
        total = chirp_sum = delay_sum = jnp.zeros((8, 256), F32)
        for o in range(GROUP):
            for k in range(2):
                mass = jnp.exp(scores[k][o] - peak)
                total = total + mass
                chirp_sum = chirp_sum + mass * fact(o, 1 + k)
                delay_sum = delay_sum + mass * fact(o, 3 + k)
        inverse = 1.0 / total
        upper = (peak + jnp.log(total), chirp_sum * inverse, delay_sum * inverse)

        scores = arrivals(16)
        peak = functools.reduce(jnp.maximum, scores)
        peak = jnp.maximum(peak[:4], peak[4:])
        peak_twice = jnp.concatenate([peak, peak], axis=0)
        total = chirp_sum = delay_sum = jnp.zeros((8, 256), F32)
        for o in range(GROUP):
            mass = jnp.exp(scores[o] - peak_twice)
            total = total + mass
            chirp_sum = chirp_sum + mass * jnp.where(is_first, fact(o, 1), fact(o, 2))
            delay_sum = delay_sum + mass * jnp.where(is_first, fact(o, 3), fact(o, 4))
        total, chirp_sum, delay_sum = [v[:4] + v[4:] for v in (total, chirp_sum, delay_sum)]
        inverse = 1.0 / total
        lower = (peak + jnp.log(total), chirp_sum * inverse, delay_sum * inverse)

        for i, out in enumerate((mine_log, mine_chirp, mine_delay)):
            for h in range(2):
                lanes = slice(128 * h, 128 * h + 128)
                if j == 0:
                    packet[pl.ds(24 * i + h, 8, 2), :] = upper[i][:, lanes]
                    packet[pl.ds(24 * i + 16 + h, 4, 2), :] = lower[i][:, lanes]
                else:
                    out[pl.ds(h, 8, 2), :] = upper[i][:, lanes]
                    out[pl.ds(16 + h, 4, 2), :] = lower[i][:, lanes]
        if j == 0:
            z_copy.start()

    for copy in trait_copies:
        copy.wait_send()
    for j in range(HALVES):
        for o in range(1, GROUP):
            score_copy(j, o).wait_send()
    z_copy.wait()
    for i, out in enumerate((other_log, other_chirp, other_delay)):
        out[...] = arrived[24 * i : 24 * i + 24]
    level = jnp.log(packet[72:80] + arrived[72:80])
    for i in range(3):
        log_prior[8 * i : 8 * i + 8] = level


def local(strain, inv_asd, templates, tmpl_len, weights, chirp_mass, valid):
    base, last, twist, pick = tables()
    dealt = templates.reshape(2, 2, 256, 128).transpose(0, 2, 1, 3).reshape(2, 512, 128)
    anywhere = pl.BlockSpec(memory_space=pl.ANY)
    held = pl.BlockSpec(memory_space=pltpu.VMEM)
    dma = pltpu.SemaphoreType.DMA
    ready = pl.pallas_call(
        prepare,
        out_shape=(
            pltpu.VMEM((512, 256), F32),
            pltpu.VMEM((2, 2, 128, 256), F32),
            pltpu.VMEM((1, 128), F32),
            pltpu.VMEM(base.shape, BF16),
            pltpu.VMEM(last.shape[1:], BF16),
            pltpu.VMEM(twist.shape, F32),
        ),
        in_specs=[anywhere] * 11,
        out_specs=(held,) * 6,
        scratch_shapes=[
            pltpu.SMEM((2,), jnp.int32),
            pltpu.SMEM((2,), F32),
            pltpu.SMEM((2,), F32),
            pltpu.SMEM((48,), jnp.int32),
            pltpu.VMEM((384, 128), F32),
            pltpu.VMEM((256, 128), F32),
            pltpu.VMEM((2, 512, 128), BF16),
            pltpu.VMEM(pick.shape, BF16),
            pltpu.VMEM((384, 128), F32),
            pltpu.VMEM((128, 128), F32),
            dma((12,)),
            dma((2,)),
        ],
        compiler_params=pltpu.CompilerParams(
            collective_id=0, has_side_effects=True, vmem_limit_bytes=56 * 1024 * 1024
        ),
    )(
        tmpl_len, weights, chirp_mass, valid,
        strain.reshape(384, 128), inv_asd.reshape(256, 128), dealt, base, last, twist, pick,
    )
    mine_log, mine_chirp, mine_delay, other_log, other_chirp, other_delay, log_prior = pl.pallas_call(
        match,
        out_shape=(pltpu.VMEM((24, 128), F32),) * 7,
        in_specs=[held] * 6,
        out_specs=(held,) * 7,
        scratch_shapes=[
            pltpu.VMEM((HALVES, GROUP, 24, 256), F32),
            pltpu.VMEM((HALVES, GROUP, 24, 256), F32),
            pltpu.VMEM((GROUP, 1, 128), F32),
            pltpu.VMEM((80, 128), F32),
            pltpu.VMEM((80, 128), F32),
            dma((HALVES, GROUP)),
            dma((HALVES, GROUP)),
            dma((GROUP,)),
            dma((GROUP,)),
            dma((2,)),
        ],
        compiler_params=pltpu.CompilerParams(
            collective_id=1, has_side_effects=True, vmem_limit_bytes=56 * 1024 * 1024
        ),
    )(*[pltpu.with_memory_space_constraint(array, pltpu.VMEM) for array in ready])
    peak = jnp.maximum(mine_log, other_log)
    mass_a, mass_b = jnp.exp(mine_log - peak), jnp.exp(other_log - peak)
    total = mass_a + mass_b
    outs = (
        peak + jnp.log(total) - log_prior,
        (mass_a * mine_chirp + mass_b * other_chirp) / total,
        (mass_a * mine_delay + mass_b * other_delay) / total,
    )
    return tuple(out.reshape(3072) for out in outs)


def solution(mesh):
    placed = (P("seg"), P(), P(None, "bank", None), P("bank"), P("bank"), P("bank"), P("seg"))
    return jax.shard_map(
        local,
        mesh=mesh,
        in_specs=placed,
        out_specs=(P(("seg", "bank")), P(("seg", "bank")), P(("seg", "bank"))),
        check_vma=False,
    )
```
